128 devices in a mesh: lon: 16 (over y, x_hi, core), lat: 8 (over z, x_lo).
Axes of the slice: x: 4 (x_hi: 2, x_lo: 2; x = x_hi * 2 + x_lo), y: 4, z: 4, core: 2. Of those that a mesh axis runs over, the one named last changes fastest.
Arguments:
- field: bfloat16 [78, 512, 2048], P(None, 'lat', 'lon'), may hold values from -6 to 6
- first_kernel: bfloat16 [48, 78, 5, 5], replicated, may hold values from -0.125 to 0.125
- norm_gain: float32 [48], replicated, may hold values from 0.25 to 1.75
- second_kernel: bfloat16 [78, 48, 5, 5], replicated, may hold values from -0.1875 to 0.1875
- cotangent: bfloat16 [78, 512, 2048], P(None, 'lat', 'lon'), may hold values from -6 to 6
Outputs:
- output: bfloat16 [78, 512, 2048], P(None, 'lat', 'lon')
- grad_field: bfloat16 [78, 512, 2048], P(None, 'lat', 'lon')
- grad_first: float32 [48, 78, 5, 5], replicated
- grad_second: float32 [78, 48, 5, 5], replicated
- grad_gain: float32 [48], replicated
The draws below stay inside these ranges and needn't reach their ends.
All inputs are finite; a program needn't handle non-finite values.
Results may differ from the reference program's by a relative error of at most 0.0039.
Values may be sent and summed in bfloat16 or wider, within the bound.
No kernel may reach another device: no remote copies, remote signals or barrier semaphores. Data moves between devices by JAX's collectives and lax.ppermute only.
A program may use at most 128 MiB of HBM per device.

```python
import jax
import jax.numpy as jnp
from jax import lax

C_IN = 78
HID = 48
NLAT = 512
NLON = 2048


def steps_of(key, extent, pieces, low, top_value):
    def one(dim, blocks):
        steps = jax.random.uniform(jax.random.fold_in(jax.random.fold_in(key, 6), dim), (blocks,), jnp.float32, low / len(pieces), top_value / len(pieces))
        return jnp.repeat(jnp.exp(steps), extent[dim] // blocks).reshape((-1,) + (1,) * (len(extent) - dim - 1))

    gain = one(*pieces[0])
    for cut in pieces[1:]:
        gain = gain * one(*cut)
    return gain


def bell_draw(stream_key, shape, deviation, reach, split=(), kind=jnp.bfloat16):
    values = jax.random.normal(stream_key, shape, jnp.float32) * deviation
    if len(split) > 0:
        values = steps_of(stream_key, shape, split, -0.22, 0.18) * values
    return jnp.clip(values, min=-reach, max=reach).astype(kind)


def setup_inputs(seed: int = 0) -> dict:
    keys = jax.random.split(jax.random.key(seed), 6)
    return {
        "field": bell_draw(keys[0], (C_IN, NLAT, NLON), 1.0, 6.0, ((1, 8), (2, 16))),
        "first_kernel": bell_draw(keys[1], (HID, C_IN, 5, 5), (C_IN * 25) ** -0.5, 0.125),
        "norm_gain": jnp.clip(1.0 + 0.15 * jax.random.normal(keys[2], (HID,), jnp.float32), 0.25, 1.75),
        "second_kernel": bell_draw(keys[3], (C_IN, HID, 5, 5), (HID * 25) ** -0.5, 0.1875),
        "cotangent": bell_draw(keys[4], (C_IN, NLAT, NLON), 1.0, 6.0, ((1, 8), (2, 16))),
    }


EPS = 1e-05

def conv_valid(padded, kernel):
    return lax.conv_general_dilated(padded[None], kernel, (1, 1), 'VALID', dimension_numbers=('NCHW', 'OIHW', 'NCHW'), preferred_element_type=jnp.float32)[0]

def conv_back(grad, kernel):
    wide = jnp.pad(grad, ((0, 0), (4, 4), (4, 4)))
    turned = jnp.transpose(kernel, (1, 0, 2, 3))[:, :, ::-1, ::-1]
    return conv_valid(wide, turned)

def kernel_grad(padded, grad):
    result = lax.conv_general_dilated(padded[None], grad[None], (1, 1), 'VALID', dimension_numbers=('CNHW', 'IOHW', 'NCHW'), preferred_element_type=jnp.float32)
    return jnp.transpose(result, (1, 0, 2, 3))

def pad_global(field):
    half = field.shape[2] // 2
    height = field.shape[1]
    top = jnp.roll(field[:, 1::-1], half, axis=2)
    bottom = jnp.roll(field[:, height - 1:height - 3:-1], half, axis=2)
    tall = jnp.concatenate([top, field, bottom], axis=1)
    return jnp.concatenate([tall[:, :, -2:], tall, tall[:, :, :2]], axis=2)

def pad_adjoint(grown):
    shape = (grown.shape[0], grown.shape[1] - 4, grown.shape[2] - 4)
    unused, backward = jax.vjp(pad_global, jnp.zeros(shape, jnp.float32))
    return backward(grown)[0]

def reference(field, first_kernel, norm_gain, second_kernel, cotangent):
    padded_in = pad_global(field)
    pre = conv_valid(padded_in, first_kernel)
    scale = lax.rsqrt(lax.optimization_barrier(jnp.mean(pre * pre, axis=0, keepdims=True)) + EPS)
    normed = pre * scale * norm_gain[:, None, None]
    active = jax.nn.silu(normed).astype(jnp.bfloat16)
    padded_act = pad_global(active)
    output = (field.astype(jnp.float32) + conv_valid(padded_act, second_kernel)).astype(jnp.bfloat16)
    grad_act = pad_adjoint(conv_back(cotangent, second_kernel))
    second_total = kernel_grad(padded_act, cotangent)
    sig = jax.nn.sigmoid(normed)
    grad_normed = grad_act * sig * (1.0 + normed * (1.0 - sig))
    gain_total = lax.optimization_barrier(jnp.sum(grad_normed * pre * scale, axis=(1, 2)))
    scaled = grad_normed * norm_gain[:, None, None]
    grad_pre = scale * scaled - pre * (scale * scale * scale) * lax.optimization_barrier(jnp.mean(scaled * pre, axis=0, keepdims=True))
    grad_pre = grad_pre.astype(jnp.bfloat16)
    first_total = kernel_grad(padded_in, grad_pre)
    grad_field = (cotangent.astype(jnp.float32) + pad_adjoint(conv_back(grad_pre, first_kernel))).astype(jnp.bfloat16)
    factor = 1.0 / jnp.sqrt(jnp.float32(NLAT * NLON))
    return (output, grad_field, first_total * factor, second_total * factor, gain_total * factor)
```

```python
import functools

import jax
import jax.numpy as jnp
from jax import lax
from jax.experimental import pallas as pl
from jax.experimental.pallas import tpu as pltpu
from jax.sharding import PartitionSpec as P

EPS = 1e-05
BF = jnp.bfloat16
F32 = jnp.float32
AXES = ("lon", "lat")
CP = 80
VMEM = 56 * 1024 * 1024


def dot(a, b):
    return jnp.dot(a, b, preferred_element_type=F32)


def dot_nt(a, b):
    return lax.dot_general(a, b, (((1,), (1,)), ((), ())), preferred_element_type=F32)


def lanes_of(shape):
    return lax.broadcasted_iota(jnp.int32, shape, len(shape) - 1)


def edge_columns(read, rows, channels):
    pair = lanes_of((channels, 128)) // 2

    def body(r, found):
        low, high = found
        x = read(r)
        low = jnp.where(pair == r, pltpu.roll(x, 2 * r, 1), low)
        high = jnp.where(pair == r, pltpu.roll(x, lax.rem(2 * r + 2, 128), 1), high)
        return low, high

    zero = jnp.zeros((channels, 128), BF)
    return lax.fori_loop(0, rows, body, (zero, zero))


def shifted(x, right, left, row):
    lane = lanes_of(x.shape)
    back = lax.rem(128 - 2 * row, 128)
    right = pltpu.roll(right, back, 1)
    left = pltpu.roll(left, lax.rem(254 - 2 * row, 128), 1)
    return [
        pltpu.roll(jnp.where(lane >= 126, left, x), 2, 1),
        pltpu.roll(jnp.where(lane >= 127, left, x), 1, 1),
        x,
        pltpu.roll(jnp.where(lane < 1, right, x), 127, 1),
        pltpu.roll(jnp.where(lane < 2, right, x), 126, 1),
    ]


def store_shifted(out, at, x, right, left, row):
    c = x.shape[0]
    for q, piece in enumerate(shifted(x, right, left, row)):
        out[at, q * c : (q + 1) * c, :] = piece


def fill_shifted(out, read_main, right, left, rows, halo):
    def body(r, carry):
        store_shifted(out, r + 2, read_main(r), right(), left(), r)
        return carry

    lax.fori_loop(0, rows, body, 0)
    for at, x, far_right, far_left, row in halo:
        store_shifted(out, at, x, far_right, far_left, row)


def wide(ref, start, count):
    return jnp.concatenate([ref[start + t] for t in range(count)], axis=1)


def add_taps(acc, start, y, m, count, flip=None):
    for t in range(count):
        cols = slice(t * 128, (t + 1) * 128)
        for p in range(5):
            part = y[p * m : (p + 1) * m, cols]
            if flip is not None:
                part = jnp.where(flip[t], y[(4 - p) * m : (5 - p) * m, cols], part)
            acc[start[t] + 4 - p] = acc[start[t] + 4 - p] + part


def conv_rows(acc, stack, weight, m, rows, flip=None):
    acc[...] = jnp.zeros(acc.shape, F32)

    def body(i, carry):
        first = 2 + 4 * i
        y = dot(weight[...], wide(stack, first, 4))
        add_taps(acc, [first + t for t in range(4)], y, m, 4)
        return carry

    lax.fori_loop(0, rows // 4, body, 0)
    outer = (0, 1, rows + 2, rows + 3)
    y = dot(weight[...], jnp.concatenate([stack[i] for i in outer], axis=1))
    add_taps(acc, outer, y, m, 4, flip)


def row_stack(ref, i):
    return ref[pl.ds(i, 5)].reshape(5 * ref.shape[1], 128)


def correlate(stack, grown, rows, flip=None):
    n = 5 * grown.shape[1]

    def body(i, total):
        first = 2 + 4 * i
        right = jnp.concatenate([row_stack(grown, first + t) for t in range(4)], axis=1)
        return total + dot_nt(wide(stack, first, 4), right)

    total = lax.fori_loop(0, rows // 4, body, jnp.zeros((stack.shape[1], n), F32))
    outer = (0, 1, rows + 2, rows + 3)
    pieces = []
    for t, i in enumerate(outer):
        piece = row_stack(grown, i)
        if flip is not None:
            turned = jnp.concatenate([grown[i + 4 - m] for m in range(5)], axis=0)
            piece = jnp.where(flip[t], turned, piece)
        pieces.append(piece)
    left = jnp.concatenate([stack[i] for i in outer], axis=1)
    return total + dot_nt(left, jnp.concatenate(pieces, axis=1))


def pack_kernel(rows_ref, field, cot, main, low, high, rim_1, rim_2):
    height = field.shape[1]
    lost = CP - field.shape[0]
    for which, source in enumerate((field, cot)):
        for b in range(height // 16):
            block = source[:, b * 16 : (b + 1) * 16, :].astype(F32)
            block = jnp.concatenate([block, jnp.zeros((lost, 16, 128), F32)], axis=0)
            main[which, b * 16 : (b + 1) * 16] = jnp.swapaxes(block, 0, 1).astype(BF)
        low[which], high[which] = edge_columns(lambda r: main[which, r], height, CP)
        for t in range(2):
            rim_1[which, t] = main[which, rows_ref[t]]
            rim_2[which, t] = main[which, rows_ref[2 + t]]


def halo_slabs(rows_ref, odd, rim_1, rim_2, far_1, far_2, which, lo, hi):
    got = []
    for side in range(2):
        upper = side == 0
        pick = odd if upper else jnp.logical_not(odd)
        far = [jnp.where(pick, far_1[which, k], far_2[which, k]) for k in range(2)]
        for t in range(2):
            slab = jnp.where(pick, rim_1[which, t], rim_2[which, t])
            got.append((slab, far[0], far[1], rows_ref[4 + 2 * side + t]))
    return got


def first_kernel_body(
    rows_ref, main, right, left, rim_1, rim_2, far_1, far_2, w_1, w_2, gain,
    both, low, high, out_1, out_2, grads, gain_grad,
    stack_1, stack_2, acc_1, acc_2, grown_1, grown_2,
):
    height = main.shape[1]
    hid = gain.shape[0]
    odd = rows_ref[8] == 1
    top = rows_ref[9] == 1
    bottom = rows_ref[10] == 1
    flip = (top, top, bottom, bottom)
    outer = (0, 1, height + 2, height + 3)
    for which, stack in enumerate((stack_1, stack_2)):
        halo = halo_slabs(rows_ref, odd, rim_1, rim_2, far_1, far_2, which, None, None)
        fill_shifted(
            stack, lambda r: main[which, r], lambda: right[which], lambda: left[which], height,
            [(outer[t],) + halo[t] for t in range(4)],
        )
    conv_rows(acc_1, stack_1, w_1, hid, height)
    conv_rows(acc_2, stack_2, w_2, hid, height, flip)
    for grown in (grown_1, grown_2):
        grown[0:4] = jnp.zeros((4, hid, 128), BF)
        grown[height + 4 : height + 8] = jnp.zeros((4, hid, 128), BF)
    spread = jnp.broadcast_to(gain[...], (hid, 128))

    def cells(r, total):
        pre = acc_1[r + 4]
        grad_act = acc_2[r + 4]
        scale = lax.rsqrt(jnp.mean(pre * pre, axis=0, keepdims=True) + EPS)
        unit = pre * scale
        normed = unit * spread
        sig = 1.0 / (1.0 + jnp.exp(-normed))
        active = (normed * sig).astype(BF)
        grad_normed = grad_act * sig * (1.0 + normed * (1.0 - sig))
        g2 = grad_normed * spread
        mean = jnp.mean(g2 * pre, axis=0, keepdims=True)
        grad_pre = (scale * g2 - pre * (scale * scale * scale * mean)).astype(BF)
        grown_1[r + 4] = grad_pre
        grown_2[r + 4] = active
        both[r, 0:hid] = active
        both[r, hid : 2 * hid] = grad_pre
        return total + grad_normed * unit

    total = lax.fori_loop(0, height, cells, jnp.zeros((hid, 128), F32))
    gain_grad[...] = jnp.broadcast_to(jnp.sum(total, axis=1, keepdims=True), (hid, 128))
    low[...], high[...] = edge_columns(lambda r: both[r], height, 2 * hid)
    for t in range(2):
        out_1[t] = both[rows_ref[t]]
        out_2[t] = both[rows_ref[2 + t]]
    n = 5 * hid
    grads[0, :, 0:n] = correlate(stack_1, grown_1, height)
    grads[1, :, 0:n] = correlate(stack_2, grown_2, height, flip)


def second_kernel_body(
    rows_ref, both, right, left, rim_1, rim_2, far_1, far_2, w_1, w_2, field, cot,
    output, grad_field, stack, acc,
):
    height = field.shape[1]
    channels = field.shape[0]
    hid = both.shape[1] // 2
    odd = rows_ref[8] == 1
    top = rows_ref[9] == 1
    bottom = rows_ref[10] == 1
    outer = (0, 1, height + 2, height + 3)
    for which, (weight, base, out) in enumerate(
        ((w_1, field, output), (w_2, cot, grad_field))
    ):
        part = slice(which * hid, (which + 1) * hid)
        halo = []
        for side in range(2):
            pick = odd if side == 0 else jnp.logical_not(odd)
            far = [jnp.where(pick, far_1[k, part], far_2[k, part]) for k in range(2)]
            for t in range(2):
                slab = jnp.where(pick, rim_1[t, part], rim_2[t, part])
                halo.append((outer[2 * side + t], slab, far[0], far[1], rows_ref[4 + 2 * side + t]))
        fill_shifted(
            stack, lambda r: both[r, part], lambda: right[part], lambda: left[part], height, halo
        )
        flip = (top, top, bottom, bottom) if which == 1 else None
        conv_rows(acc, stack, weight, CP, height, flip)
        for b in range(height // 16):
            rows = slice(b * 16, (b + 1) * 16)
            block = jnp.swapaxes(acc[b * 16 + 4 : b * 16 + 20], 0, 1)[0:channels]
            out[:, rows, :] = (base[:, rows, :].astype(F32) + block).astype(BF)


def call(body, outs, scratch, args, flops):
    in_specs = [pl.BlockSpec(memory_space=pltpu.SMEM)]
    in_specs += [pl.BlockSpec(memory_space=pltpu.VMEM)] * (len(args) - 1)
    return pl.pallas_call(
        body,
        out_shape=[jax.ShapeDtypeStruct(s, t) for s, t in outs],
        in_specs=in_specs,
        out_specs=[pl.BlockSpec(memory_space=pltpu.VMEM)] * len(outs),
        scratch_shapes=[pltpu.VMEM(s, t) for s, t in scratch],
        compiler_params=pltpu.CompilerParams(vmem_limit_bytes=VMEM),
        cost_estimate=pl.CostEstimate(flops=flops, bytes_accessed=8 << 20, transcendentals=0),
    )(*args)


def exchange_columns(low, high):
    count = lax.axis_size("lon")
    up = [(i, (i + 1) % count) for i in range(count)]
    down = [(t, s) for s, t in up]
    right = lax.ppermute(low, "lon", down)
    left = lax.ppermute(high, "lon", up)
    return right, left


def row_routes(lon, lat):
    def at(x, y):
        return (x % lon) * lat + y

    one, two = [], []
    for x in range(lon):
        for y in range(lat):
            one.append((at(x, y), at(x, y + 1 if y % 2 == 0 else y - 1)))
            if y == 0 or y == lat - 1:
                two.append((at(x, y), at(x + lon // 2, y)))
            else:
                two.append((at(x, y), at(x, y - 1 if y % 2 == 0 else y + 1)))
    return one, two


def place_numbers(height):
    lat = lax.axis_index("lat")
    last = lax.axis_size("lat") - 1
    odd = lat % 2
    top = (lat == 0).astype(jnp.int32)
    bottom = (lat == last).astype(jnp.int32)
    h = height
    send_1 = [jnp.where(odd == 1, 0, h - 2), jnp.where(odd == 1, 1, h - 1)]
    send_2 = [
        jnp.where(odd == 1, h - 2 + bottom, top),
        jnp.where(odd == 1, h - 1 - bottom, 1 - top),
    ]
    got = [
        jnp.where(top == 1, 1, h - 2),
        jnp.where(top == 1, 0, h - 1),
        jnp.where(bottom == 1, h - 1, 0),
        jnp.where(bottom == 1, h - 2, 1),
    ]
    values = send_1 + send_2 + got + [odd, top, bottom]
    return jnp.stack([jnp.asarray(v, jnp.int32) for v in values])


def grown_sum(flat):
    got = lax.all_to_all(flat, AXES, 0, 0)
    total = jnp.sum(got.astype(F32), axis=0)
    return total


def taps(kernel, order, pads):
    out = jnp.transpose(kernel, order)
    return jnp.pad(out, pads)


def per_device(field, first_kernel, norm_gain, second_kernel, cotangent):
    channels, height, width = field.shape
    hid = norm_gain.shape[0]
    devices = lax.axis_size("lon") * lax.axis_size("lat")
    lost = CP - channels
    numbers = place_numbers(height)
    one, two = row_routes(lax.axis_size("lon"), lax.axis_size("lat"))
    flops = 2 * height * 128 * 25 * channels * hid

    main, low, high, rim_1, rim_2 = call(
        pack_kernel,
        [
            ((2, height, CP, 128), BF), ((2, CP, 128), BF), ((2, CP, 128), BF),
            ((2, 2, CP, 128), BF), ((2, 2, CP, 128), BF),
        ],
        [],
        (numbers, field, cotangent),
        flops // 8,
    )
    right, left = exchange_columns(low, high)
    sides = jnp.stack([right, left], axis=1)
    rim_1, far_1 = lax.ppermute((rim_1, sides), AXES, one)
    rim_2, far_2 = lax.ppermute((rim_2, sides), AXES, two)

    def flipped(k):
        return k[:, :, ::-1, ::-1]

    w_1 = taps(first_kernel, (2, 0, 3, 1), ((0, 0), (0, 0), (0, 0), (0, lost))).reshape(5 * hid, 5 * CP)
    w_2 = taps(flipped(second_kernel), (2, 1, 3, 0), ((0, 0), (0, 0), (0, 0), (0, lost))).reshape(5 * hid, 5 * CP)
    w_3 = taps(second_kernel, (2, 0, 3, 1), ((0, 0), (0, lost), (0, 0), (0, 0))).reshape(5 * CP, 5 * hid)
    w_4 = taps(flipped(first_kernel), (2, 1, 3, 0), ((0, 0), (0, lost), (0, 0), (0, 0))).reshape(5 * CP, 5 * hid)

    both, low, high, out_1, out_2, grads, gain_grad = call(
        first_kernel_body,
        [
            ((height, 2 * hid, 128), BF), ((2 * hid, 128), BF), ((2 * hid, 128), BF),
            ((2, 2 * hid, 128), BF), ((2, 2 * hid, 128), BF),
            ((2, 5 * CP, 256), F32), ((hid, 128), F32),
        ],
        [
            ((height + 4, 5 * CP, 128), BF), ((height + 4, 5 * CP, 128), BF),
            ((height + 8, hid, 128), F32), ((height + 8, hid, 128), F32),
            ((height + 8, hid, 128), BF), ((height + 8, hid, 128), BF),
        ],
        (numbers, main, right, left, rim_1, rim_2, far_1, far_2, w_1, w_2, norm_gain[:, None]),
        4 * flops,
    )

    n = 5 * hid
    rows = -(-(2 * 5 * CP * 2 + hid) // (16 * devices)) * 16
    flat = jnp.concatenate(
        [
            grads[:, :, 0:128].reshape(-1, 128),
            jnp.pad(grads[:, :, 128:n], ((0, 0), (0, 0), (0, 256 - n))).reshape(-1, 128),
            gain_grad,
        ],
        axis=0,
    )
    flat = jnp.pad(flat, ((0, rows * devices - flat.shape[0]), (0, 0))).astype(BF)
    got = lax.all_to_all(flat.reshape(devices, rows, 128), AXES, 0, 0)
    factor = 1.0 / jnp.sqrt(F32(height * width * devices))
    mine = (jnp.sum(got.astype(F32), axis=0) * factor).astype(BF)
    all_rows = lax.all_to_all(jnp.broadcast_to(mine, (devices, rows, 128)), AXES, 0, 0)
    all_rows = all_rows.reshape(-1, 128)

    right, left = exchange_columns(low, high)
    sides = jnp.stack([right, left], axis=0)
    out_1, far_1 = lax.ppermute((out_1, sides), AXES, one)
    out_2, far_2 = lax.ppermute((out_2, sides), AXES, two)
    output, grad_field = call(
        second_kernel_body,
        [(field.shape, BF), (field.shape, BF)],
        [((height + 4, 5 * hid, 128), BF), ((height + 8, CP, 128), F32)],
        (numbers, both, right, left, out_1, out_2, far_1, far_2, w_3, w_4, field, cotangent),
        2 * flops,
    )

    size = 2 * 5 * CP
    sums = jnp.concatenate(
        [all_rows[0:size], all_rows[size : 2 * size, 0 : n - 128]], axis=1
    ).astype(F32).reshape(2, 5, CP, 5, hid)[:, :, 0:channels]
    grad_first = jnp.transpose(sums[0], (3, 1, 2, 0))[:, :, ::-1, :]
    grad_second = jnp.transpose(sums[1], (1, 3, 2, 0))[:, :, :, ::-1]
    grad_gain = all_rows[2 * size : 2 * size + hid, 0].astype(F32)
    return output, grad_field, grad_first, grad_second, grad_gain


def solution(mesh):
    placed = (P(None, "lat", "lon"), P(), P(), P(), P(None, "lat", "lon"))
    return jax.shard_map(
        per_device,
        mesh=mesh,
        in_specs=placed,
        out_specs=(P(None, "lat", "lon"), P(None, "lat", "lon"), P(), P(), P()),
        check_vma=False,
    )
```

```python
import functools

import jax
import jax.numpy as jnp
from jax import lax
from jax.experimental import pallas as pl
from jax.experimental.pallas import tpu as pltpu
from jax.sharding import PartitionSpec as P

EPS = 1e-05
BF = jnp.bfloat16
F32 = jnp.float32
AXES = ("lon", "lat")
CP = 80
WIRE = BF
VMEM = 56 * 1024 * 1024


def dot(a, b):
    return jnp.dot(a, b, preferred_element_type=F32)


def dot_nt(a, b):
    return lax.dot_general(a, b, (((1,), (1,)), ((), ())), preferred_element_type=F32)


def lanes_of(shape):
    return lax.broadcasted_iota(jnp.int32, shape, len(shape) - 1)


def edge_columns(read, rows, channels):
    pair = lanes_of((channels, 128)) // 2

    def body(r, found):
        low, high = found
        x = read(r)
        low = jnp.where(pair == r, pltpu.roll(x, 2 * r, 1), low)
        high = jnp.where(pair == r, pltpu.roll(x, lax.rem(2 * r + 2, 128), 1), high)
        return low, high

    zero = jnp.zeros((channels, 128), BF)
    return lax.fori_loop(0, rows, body, (zero, zero), unroll=16)


def shifted(x, right, left, row):
    lane = lanes_of(x.shape)
    back = lax.rem(128 - 2 * row, 128)
    right = pltpu.roll(right, back, 1)
    left = pltpu.roll(left, lax.rem(254 - 2 * row, 128), 1)
    return [
        pltpu.roll(jnp.where(lane >= 126, left, x), 2, 1),
        pltpu.roll(jnp.where(lane >= 127, left, x), 1, 1),
        x,
        pltpu.roll(jnp.where(lane < 1, right, x), 127, 1),
        pltpu.roll(jnp.where(lane < 2, right, x), 126, 1),
    ]


def store_shifted(out, at, x, right, left, row):
    c = x.shape[0]
    for q, piece in enumerate(shifted(x, right, left, row)):
        out[at, q * c : (q + 1) * c, :] = piece


def fill_shifted(out, read_main, right, left, rows, halo):
    def body(r, carry):
        store_shifted(out, r + 2, read_main(r), right(), left(), r)
        return carry

    lax.fori_loop(0, rows, body, 0, unroll=4)
    for at, x, far_right, far_left, row in halo:
        store_shifted(out, at, x, far_right, far_left, row)


def wide(ref, start, count):
    return jnp.concatenate([ref[start + t] for t in range(count)], axis=1)


def add_taps(acc, start, y, m, count, flip=None):
    for t in range(count):
        cols = slice(t * 128, (t + 1) * 128)
        for p in range(5):
            part = y[p * m : (p + 1) * m, cols]
            if flip is not None:
                part = jnp.where(flip[t], y[(4 - p) * m : (5 - p) * m, cols], part)
            acc[start[t] + 4 - p] = acc[start[t] + 4 - p] + part


def conv_rows(acc, stack, weight, m, rows, flip=None):
    acc[...] = jnp.zeros(acc.shape, F32)

    y = dot(weight[...], wide(stack, 2, rows))
    add_taps(acc, range(2, rows + 2), y, m, rows)
    outer = (0, 1, rows + 2, rows + 3)
    y = dot(weight[...], jnp.concatenate([stack[i] for i in outer], axis=1))
    add_taps(acc, outer, y, m, 4, flip)


def row_stack(ref, i):
    return ref[pl.ds(i, 5)].reshape(5 * ref.shape[1], 128)


def correlate(stack, grown, rows, flip=None):
    inner = range(2, rows + 2)
    right = jnp.concatenate([row_stack(grown, i) for i in inner], axis=1)
    total = dot_nt(wide(stack, 2, rows), right)
    outer = (0, 1, rows + 2, rows + 3)
    pieces = []
    for t, i in enumerate(outer):
        piece = row_stack(grown, i)
        if flip is not None:
            turned = jnp.concatenate([grown[i + 4 - m] for m in range(5)], axis=0)
            piece = jnp.where(flip[t], turned, piece)
        pieces.append(piece)
    left = jnp.concatenate([stack[i] for i in outer], axis=1)
    return total + dot_nt(left, jnp.concatenate(pieces, axis=1))


def pack_kernel(rows_ref, field, cot, main, low, high, rim_1, rim_2):
    height = field.shape[1]
    lost = CP - field.shape[0]
    for which, source in enumerate((field, cot)):
        for b in range(height // 16):
            block = source[:, b * 16 : (b + 1) * 16, :].astype(F32)
            block = jnp.concatenate([block, jnp.zeros((lost, 16, 128), F32)], axis=0)
            main[which, b * 16 : (b + 1) * 16] = jnp.swapaxes(block, 0, 1).astype(BF)
        low[which], high[which] = edge_columns(lambda r: main[which, r], height, CP)
        for t in range(2):
            rim_1[which, t] = main[which, rows_ref[t]]
            rim_2[which, t] = main[which, rows_ref[2 + t]]


def halo_slabs(rows_ref, odd, rim_1, rim_2, far_1, far_2, which, lo, hi):
    got = []
    for side in range(2):
        upper = side == 0
        pick = odd if upper else jnp.logical_not(odd)
        far = [jnp.where(pick, far_1[which, k], far_2[which, k]) for k in range(2)]
        for t in range(2):
            slab = jnp.where(pick, rim_1[which, t], rim_2[which, t])
            got.append((slab, far[0], far[1], rows_ref[4 + 2 * side + t]))
    return got


def first_kernel_body(
    rows_ref, main, right, left, rim_1, rim_2, far_1, far_2, w_1, w_2, gain,
    both, low, high, out_1, out_2, flat,
    stack_1, stack_2, acc_1, acc_2, grown_1, grown_2,
):
    height = main.shape[1]
    hid = gain.shape[0]
    odd = rows_ref[8] == 1
    top = rows_ref[9] == 1
    bottom = rows_ref[10] == 1
    flip = (top, top, bottom, bottom)
    outer = (0, 1, height + 2, height + 3)
    for which, stack in enumerate((stack_1, stack_2)):
        halo = halo_slabs(rows_ref, odd, rim_1, rim_2, far_1, far_2, which, None, None)
        fill_shifted(
            stack, lambda r: main[which, r], lambda: right[which], lambda: left[which], height,
            [(outer[t],) + halo[t] for t in range(4)],
        )
    conv_rows(acc_1, stack_1, w_1, hid, height)
    conv_rows(acc_2, stack_2, w_2, hid, height, flip)
    for grown in (grown_1, grown_2):
        grown[0:4] = jnp.zeros((4, hid, 128), BF)
        grown[height + 4 : height + 8] = jnp.zeros((4, hid, 128), BF)
    spread = jnp.broadcast_to(gain[...], (hid, 128))

    def cells(r, total):
        pre = acc_1[r + 4]
        grad_act = acc_2[r + 4]
        scale = lax.rsqrt(jnp.mean(pre * pre, axis=0, keepdims=True) + EPS)
        unit = pre * scale
        normed = unit * spread
        sig = 1.0 / (1.0 + jnp.exp(-normed))
        active = (normed * sig).astype(BF)
        grad_normed = grad_act * sig * (1.0 + normed * (1.0 - sig))
        g2 = grad_normed * spread
        mean = jnp.mean(g2 * pre, axis=0, keepdims=True)
        grad_pre = (scale * g2 - pre * (scale * scale * scale * mean)).astype(BF)
        grown_1[r + 4] = grad_pre
        grown_2[r + 4] = active
        both[r, 0:hid] = active
        both[r, hid : 2 * hid] = grad_pre
        return total + grad_normed * unit

    total = lax.fori_loop(0, height, cells, jnp.zeros((hid, 128), F32), unroll=4)
    low[...], high[...] = edge_columns(lambda r: both[r], height, 2 * hid)
    for t in range(2):
        out_1[t] = both[rows_ref[t]]
        out_2[t] = both[rows_ref[2 + t]]
    m = 5 * CP
    spare = jnp.zeros((m, 256 - 5 * hid), F32)
    for which, found in enumerate(
        (correlate(stack_1, grown_1, height), correlate(stack_2, grown_2, height, flip))
    ):
        found = jnp.concatenate([found, spare], axis=1).astype(WIRE)
        flat[2 * which * m : (2 * which + 1) * m] = found[:, 0:128]
        flat[(2 * which + 1) * m : (2 * which + 2) * m] = found[:, 128:256]
    used = flat.shape[0] - 4 * m
    total = jnp.broadcast_to(jnp.sum(total, axis=1, keepdims=True), (hid, 128))
    total = jnp.concatenate([total, jnp.zeros((used - hid, 128), F32)], axis=0)
    flat[4 * m :] = total.astype(WIRE)


def second_kernel_body(
    which, rows_ref, both, right, left, rim_1, rim_2, far_1, far_2, weight, base, out, stack, acc,
):
    height = base.shape[1]
    channels = base.shape[0]
    hid = both.shape[1] // 2
    odd = rows_ref[8] == 1
    top = rows_ref[9] == 1
    bottom = rows_ref[10] == 1
    outer = (0, 1, height + 2, height + 3)
    part = slice(which * hid, (which + 1) * hid)
    halo = []
    for side in range(2):
        pick = odd if side == 0 else jnp.logical_not(odd)
        far = [jnp.where(pick, far_1[k, part], far_2[k, part]) for k in range(2)]
        for t in range(2):
            slab = jnp.where(pick, rim_1[t, part], rim_2[t, part])
            halo.append((outer[2 * side + t], slab, far[0], far[1], rows_ref[4 + 2 * side + t]))
    fill_shifted(
        stack, lambda r: both[r, part], lambda: right[part], lambda: left[part], height, halo
    )
    flip = (top, top, bottom, bottom) if which == 1 else None
    conv_rows(acc, stack, weight, CP, height, flip)
    for b in range(height // 16):
        rows = slice(b * 16, (b + 1) * 16)
        block = jnp.swapaxes(acc[b * 16 + 4 : b * 16 + 20], 0, 1)[0:channels]
        out[:, rows, :] = (base[:, rows, :].astype(F32) + block).astype(BF)


def weights_kernel(k_1, k_2, w_1, w_2, w_3, w_4):
    hid, channels = k_1.shape[2:]
    gap = jnp.zeros((hid, CP - channels), F32)

    def plane(k, p, q):
        return jnp.concatenate([k[p, q].astype(F32), gap], axis=1)

    for p in range(5):
        rows = slice(p * hid, (p + 1) * hid)
        w_1[rows] = jnp.concatenate([plane(k_1, p, q) for q in range(5)], axis=1).astype(BF)
        w_2[rows] = jnp.concatenate([plane(k_2, 4 - p, 4 - q) for q in range(5)], axis=1).astype(BF)
        rows = slice(p * CP, (p + 1) * CP)
        w_3[rows] = jnp.concatenate([plane(k_2, p, q) for q in range(5)], axis=0).T.astype(BF)
        w_4[rows] = jnp.concatenate([plane(k_1, 4 - p, 4 - q) for q in range(5)], axis=0).T.astype(BF)


def reduce_kernel(factor, got, out):
    devices = got.shape[0]

    def body(i, total):
        return total + got[i].astype(F32)

    total = lax.fori_loop(0, devices, body, jnp.zeros(got.shape[1:], F32), unroll=16)
    mine = (total * factor).astype(BF)
    for i in range(devices):
        out[i] = mine


def unpack_kernel(rows, grad_1, grad_2, gain):
    hid, channels = grad_1.shape[2:]
    m = 5 * CP
    for which in range(2):
        at = 2 * which * m
        low = rows[at : at + m].astype(F32).T
        high = rows[at + m : at + 2 * m].astype(F32).T
        both = jnp.concatenate([low, high], axis=0)
        for q in range(5):
            part = both[0 : 5 * hid, q * CP : q * CP + channels]
            for t in range(5):
                piece = part[t * hid : (t + 1) * hid]
                if which == 0:
                    grad_1[4 - t, q] = piece
                else:
                    grad_2[t, 4 - q] = piece
    gain[...] = rows[4 * m : 4 * m + hid].astype(F32).T[0:1]


def call(body, outs, scratch, args, flops, numbers=True):
    vmem = pl.BlockSpec(memory_space=pltpu.VMEM)
    in_specs = [vmem] * len(args)
    if numbers:
        in_specs[0] = pl.BlockSpec(memory_space=pltpu.SMEM)
    return pl.pallas_call(
        body,
        out_shape=[jax.ShapeDtypeStruct(s, t) for s, t in outs],
        in_specs=in_specs,
        out_specs=[vmem] * len(outs),
        scratch_shapes=[pltpu.VMEM(s, t) for s, t in scratch],
        compiler_params=pltpu.CompilerParams(vmem_limit_bytes=VMEM),
        cost_estimate=pl.CostEstimate(flops=flops, bytes_accessed=1 << 20, transcendentals=0),
    )(*args)


def exchange_columns(low, high):
    count = lax.axis_size("lon")
    up = [(i, (i + 1) % count) for i in range(count)]
    down = [(t, s) for s, t in up]
    right = lax.ppermute(low, "lon", down)
    left = lax.ppermute(high, "lon", up)
    return right, left


def row_routes(lon, lat):
    def at(x, y):
        return (x % lon) * lat + y

    one, two = [], []
    for x in range(lon):
        for y in range(lat):
            one.append((at(x, y), at(x, y + 1 if y % 2 == 0 else y - 1)))
            if y == 0 or y == lat - 1:
                two.append((at(x, y), at(x + lon // 2, y)))
            else:
                two.append((at(x, y), at(x, y - 1 if y % 2 == 0 else y + 1)))
    return one, two


def place_numbers(height):
    lat = lax.axis_index("lat")
    last = lax.axis_size("lat") - 1
    odd = lat % 2
    top = (lat == 0).astype(jnp.int32)
    bottom = (lat == last).astype(jnp.int32)
    h = height
    send_1 = [jnp.where(odd == 1, 0, h - 2), jnp.where(odd == 1, 1, h - 1)]
    send_2 = [
        jnp.where(odd == 1, h - 2 + bottom, top),
        jnp.where(odd == 1, h - 1 - bottom, 1 - top),
    ]
    got = [
        jnp.where(top == 1, 1, h - 2),
        jnp.where(top == 1, 0, h - 1),
        jnp.where(bottom == 1, h - 1, 0),
        jnp.where(bottom == 1, h - 2, 1),
    ]
    values = send_1 + send_2 + got + [odd, top, bottom]
    return jnp.stack([jnp.asarray(v, jnp.int32) for v in values])


def per_device(field, first_kernel, norm_gain, second_kernel, cotangent):
    channels, height, width = field.shape
    hid = norm_gain.shape[0]
    devices = lax.axis_size("lon") * lax.axis_size("lat")
    numbers = place_numbers(height)
    one, two = row_routes(lax.axis_size("lon"), lax.axis_size("lat"))
    us = 10**9

    main, low, high, rim_1, rim_2 = call(
        pack_kernel,
        [
            ((2, height, CP, 128), BF), ((2, CP, 128), BF), ((2, CP, 128), BF),
            ((2, 2, CP, 128), BF), ((2, 2, CP, 128), BF),
        ],
        [],
        (numbers, field, cotangent),
        5 * us,
    )
    right, left = exchange_columns(low, high)
    sides = jnp.stack([right, left], axis=1)
    rim_1, far_1 = lax.ppermute((rim_1, sides), AXES, one)
    rim_2, far_2 = lax.ppermute((rim_2, sides), AXES, two)

    w_1, w_2, w_3, w_4 = call(
        weights_kernel,
        [((5 * hid, 5 * CP), BF)] * 2 + [((5 * CP, 5 * hid), BF)] * 2,
        [],
        (jnp.transpose(first_kernel, (2, 3, 0, 1)), jnp.transpose(second_kernel, (2, 3, 1, 0))),
        4 * us,
        numbers=False,
    )
    rows = -(-(4 * 5 * CP + hid) // (16 * devices)) * 16
    both, low, high, out_1, out_2, flat = call(
        first_kernel_body,
        [
            ((height, 2 * hid, 128), BF), ((2 * hid, 128), BF), ((2 * hid, 128), BF),
            ((2, 2 * hid, 128), BF), ((2, 2 * hid, 128), BF), ((rows * devices, 128), WIRE),
        ],
        [
            ((height + 4, 5 * CP, 128), BF), ((height + 4, 5 * CP, 128), BF),
            ((height + 8, hid, 128), F32), ((height + 8, hid, 128), F32),
            ((height + 8, hid, 128), BF), ((height + 8, hid, 128), BF),
        ],
        (numbers, main, right, left, rim_1, rim_2, far_1, far_2, w_1, w_2, norm_gain[:, None]),
        30 * us,
    )

    got = lax.all_to_all(flat.reshape(devices, rows, 128), AXES, 0, 0)
    factor = (height * width * devices) ** -0.5
    (mine,) = call(
        functools.partial(reduce_kernel, factor), [((devices, rows, 128), BF)], [], (got,), 10 * us,
        numbers=False,
    )
    summed = lax.all_to_all(mine, AXES, 0, 0).reshape(-1, 128)
    grad_1, grad_2, gain = call(
        unpack_kernel,
        [((5, 5, hid, channels), F32)] * 2 + [((1, hid), F32)],
        [],
        (summed,),
        20 * us,
        numbers=False,
    )
    grad_first = jnp.transpose(grad_1, (2, 3, 0, 1))
    grad_second = jnp.transpose(grad_2, (3, 2, 0, 1))

    right, left = exchange_columns(low, high)
    sides = jnp.stack([right, left], axis=0)
    out_1, far_1 = lax.ppermute((out_1, sides), AXES, one)
    out_2, far_2 = lax.ppermute((out_2, sides), AXES, two)
    results = []
    for which, weight, base in ((0, w_3, field), (1, w_4, cotangent)):
        results += call(
            functools.partial(second_kernel_body, which),
            [(field.shape, BF)],
            [((height + 4, 5 * hid, 128), BF), ((height + 8, CP, 128), F32)],
            (numbers, both, right, left, out_1, out_2, far_1, far_2, weight, base),
            2 * us,
        )
    return results[0], results[1], grad_first, grad_second, gain.reshape(hid)


def solution(mesh):
    placed = (P(None, "lat", "lon"), P(), P(), P(), P(None, "lat", "lon"))
    return jax.shard_map(
        per_device,
        mesh=mesh,
        in_specs=placed,
        out_specs=(P(None, "lat", "lon"), P(None, "lat", "lon"), P(), P(), P()),
        check_vma=False,
    )
```

```python
import functools

import jax
import jax.numpy as jnp
from jax import lax
from jax.experimental import pallas as pl
from jax.experimental.pallas import tpu as pltpu
from jax.sharding import PartitionSpec as P

EPS = 1e-05
BF = jnp.bfloat16
F32 = jnp.float32
AXES = ("lon", "lat")
CP = 80
WIRE = BF
VMEM = 56 * 1024 * 1024


def dot(a, b):
    return jnp.dot(a, b, preferred_element_type=F32)


def dot_nt(a, b):
    return lax.dot_general(a, b, (((1,), (1,)), ((), ())), preferred_element_type=F32)


def lanes_of(shape):
    return lax.broadcasted_iota(jnp.int32, shape, len(shape) - 1)


def edge_columns(read, rows, channels):
    pair = lanes_of((channels, 128)) // 2

    def body(r, found):
        low, high = found
        x = read(r)
        low = jnp.where(pair == r, pltpu.roll(x, 2 * r, 1), low)
        high = jnp.where(pair == r, pltpu.roll(x, lax.rem(2 * r + 2, 128), 1), high)
        return low, high

    zero = jnp.zeros((channels, 128), BF)
    return lax.fori_loop(0, rows, body, (zero, zero), unroll=rows)


def shifted(x, right, left, row):
    lane = lanes_of(x.shape)
    back = lax.rem(128 - 2 * row, 128)
    right = pltpu.roll(right, back, 1)
    left = pltpu.roll(left, lax.rem(254 - 2 * row, 128), 1)
    return [
        pltpu.roll(jnp.where(lane >= 126, left, x), 2, 1),
        pltpu.roll(jnp.where(lane >= 127, left, x), 1, 1),
        x,
        pltpu.roll(jnp.where(lane < 1, right, x), 127, 1),
        pltpu.roll(jnp.where(lane < 2, right, x), 126, 1),
    ]


def store_shifted(out, at, x, right, left, row):
    c = x.shape[0]
    for q, piece in enumerate(shifted(x, right, left, row)):
        out[at, q * c : (q + 1) * c, :] = piece


def fill_shifted(out, read_main, right, left, rows, halo):
    def body(r, carry):
        store_shifted(out, r + 2, read_main(r), right(), left(), r)
        return carry

    lax.fori_loop(0, rows, body, 0, unroll=rows)
    for at, x, far_right, far_left, row in halo:
        store_shifted(out, at, x, far_right, far_left, row)


def wide(ref, start, count):
    return jnp.concatenate([ref[start + t] for t in range(count)], axis=1)


def add_taps(acc, start, y, m, count, flip=None):
    for t in range(count):
        cols = slice(t * 128, (t + 1) * 128)
        for p in range(5):
            part = y[p * m : (p + 1) * m, cols]
            if flip is not None:
                part = jnp.where(flip[t], y[(4 - p) * m : (5 - p) * m, cols], part)
            acc[start[t] + 4 - p] = acc[start[t] + 4 - p] + part


def conv_rows(acc, stack, weight, m, rows, flip=None):
    acc[...] = jnp.zeros(acc.shape, F32)

    y = dot(weight[...], wide(stack, 2, rows))
    add_taps(acc, range(2, rows + 2), y, m, rows)
    outer = (0, 1, rows + 2, rows + 3)
    y = dot(weight[...], jnp.concatenate([stack[i] for i in outer], axis=1))
    add_taps(acc, outer, y, m, 4, flip)


def row_stack(ref, i):
    return ref[pl.ds(i, 5)].reshape(5 * ref.shape[1], 128)


def correlate_outer(outer, grown, places, flip=None):
    pieces = []
    for t, i in enumerate(places):
        piece = row_stack(grown, i)
        if flip is not None:
            turned = jnp.concatenate([grown[i + 4 - m] for m in range(5)], axis=0)
            piece = jnp.where(flip[t], turned, piece)
        pieces.append(piece)
    return dot_nt(wide(outer, 0, 4), jnp.concatenate(pieces, axis=1))


def shifted_alone(x):
    lane = lanes_of(x.shape)
    zero = jnp.zeros_like(x)
    return [
        jnp.where(lane < 2, zero, pltpu.roll(x, 2, 1)),
        jnp.where(lane < 1, zero, pltpu.roll(x, 1, 1)),
        x,
        jnp.where(lane >= 127, zero, pltpu.roll(x, 127, 1)),
        jnp.where(lane >= 126, zero, pltpu.roll(x, 126, 1)),
    ]


def four_slots(high, low):
    source = lax.broadcasted_iota(jnp.int32, (256, 256), 0)
    target = lax.broadcasted_iota(jnp.int32, (256, 256), 1)
    side = (source >= 128).astype(jnp.int32)
    place = 4 * ((source - 128 * side) // 2) + source % 2 + 2 * side
    route = (target == place).astype(F32).astype(BF)
    return dot(jnp.concatenate([high, low], axis=1), route).astype(BF)


def edge_stack(right, left):
    c = right.shape[0]
    odd = lanes_of(right.shape) % 2 == 1
    zero = jnp.zeros_like(right)
    high = [zero, zero, zero, jnp.where(odd, pltpu.roll(right, 1, 1), zero), right]
    low = [left, jnp.where(odd, zero, pltpu.roll(left, 127, 1)), zero, zero, zero]
    return four_slots(jnp.concatenate(high, axis=0), jnp.concatenate(low, axis=0))


def slid(x, rows):
    by = 4 * rows
    if by == 0:
        return x
    lane = lanes_of(x.shape)
    inside = lane >= by if by > 0 else lane < 256 + by
    return jnp.where(inside, pltpu.roll(x, by % 256, 1), jnp.zeros_like(x))


def conv_alone(main, which, stack, weight, acc):
    height = main.shape[1]

    def body(r, carry):
        for q, piece in enumerate(shifted_alone(main[which, r])):
            stack[r, q * CP : (q + 1) * CP] = piece
        return carry

    lax.fori_loop(0, height, body, 0, unroll=8)
    acc[...] = jnp.zeros(acc.shape, F32)
    y = dot(weight[...], wide(stack, 0, height))
    add_taps(acc, range(2, height + 2), y, acc.shape[1], height)


def pack_kernel(rows_ref, field, cot, main, low, high, rim_1, rim_2):
    height = field.shape[1]
    lost = CP - field.shape[0]
    for which, source in enumerate((field, cot)):
        for b in range(height // 16):
            block = source[:, b * 16 : (b + 1) * 16, :].astype(F32)
            block = jnp.concatenate([block, jnp.zeros((lost, 16, 128), F32)], axis=0)
            main[which, b * 16 : (b + 1) * 16] = jnp.swapaxes(block, 0, 1).astype(BF)
        low[which], high[which] = edge_columns(lambda r: main[which, r], height, CP)
        for t in range(2):
            rim_1[which, t] = main[which, rows_ref[t]]
            rim_2[which, t] = main[which, rows_ref[2 + t]]


def halo_slabs(rows_ref, odd, rim_1, rim_2, far_1, far_2, which):
    got = []
    for side in range(2):
        upper = side == 0
        pick = odd if upper else jnp.logical_not(odd)
        far = [jnp.where(pick, far_1[which, k], far_2[which, k]) for k in range(2)]
        for t in range(2):
            slab = jnp.where(pick, rim_1[which, t], rim_2[which, t])
            got.append((slab, far[0], far[1], rows_ref[4 + 2 * side + t]))
    return got


def first_kernel_body(
    rows_ref, main, right, left, rim_1, rim_2, far_1, far_2, w_1, w_2, gain,
    both, low, high, out_1, out_2, flat,
    stack_1, stack_2, acc_1, acc_2, grown_1, grown_2, outer_1, outer_2, edge_1, edge_2, z_1, z_2,
):
    height, _, _ = both.shape
    hid = gain.shape[0]
    odd = rows_ref[8] == 1
    top = rows_ref[9] == 1
    bottom = rows_ref[10] == 1
    flip = (top, top, bottom, bottom)
    places = (0, 1, height + 2, height + 3)
    for grown in (grown_1, grown_2):
        grown[0:4] = jnp.zeros((4, hid, 128), BF)
        grown[height + 4 : height + 8] = jnp.zeros((4, hid, 128), BF)
    weights = (w_1, w_2)
    for which, (outer, edge, z) in enumerate(((outer_1, edge_1, z_1), (outer_2, edge_2, z_2))):
        halo = halo_slabs(rows_ref, odd, rim_1, rim_2, far_1, far_2, which)
        for t in range(4):
            store_shifted(outer, t, *halo[t])
        edge[...] = edge_stack(right[which], left[which])
        y = dot(weights[which][...], edge[...])
        found = sum(slid(y[p * hid : (p + 1) * hid], 2 - p) for p in range(5))
        z[0] = found[:, 0:128]
        z[1] = found[:, 128:256]
    conv_alone(main, 0, stack_1, w_1, acc_1)
    conv_alone(main, 1, stack_2, w_2, acc_2)
    for which, (outer, acc) in enumerate(((outer_1, acc_1), (outer_2, acc_2))):
        y = dot(weights[which][...], wide(outer, 0, 4))
        add_taps(acc, places, y, hid, 4, flip if which == 1 else None)
    spread = gain[...]
    lane = lanes_of((hid, 128))
    side = jnp.logical_or(lane < 2, lane >= 126)

    def cells(r, total):
        turn = lax.rem(382 - 4 * r, 128)

        def with_edges(acc, z):
            return acc[r + 4] + jnp.where(side, pltpu.roll(z[r // 32], turn, 1), 0.0)

        pre = with_edges(acc_1, z_1)
        grad_act = with_edges(acc_2, z_2)
        scale = lax.rsqrt(jnp.mean(pre * pre, axis=0, keepdims=True) + EPS)
        unit = pre * scale
        normed = unit * spread
        sig = 1.0 / (1.0 + jnp.exp(-normed))
        active = (normed * sig).astype(BF)
        grad_normed = grad_act * sig * (1.0 + normed * (1.0 - sig))
        g2 = grad_normed * spread
        mean = jnp.mean(g2 * pre, axis=0, keepdims=True)
        grad_pre = (scale * g2 - pre * (scale * scale * scale * mean)).astype(BF)
        grown_1[r + 4] = grad_pre
        grown_2[r + 4] = active
        both[r, 0:hid] = active
        both[r, hid : 2 * hid] = grad_pre
        return total + grad_normed * unit

    total = lax.fori_loop(0, height, cells, jnp.zeros((hid, 128), F32), unroll=16)
    lows, highs = edge_columns(lambda r: both[r], height, 2 * hid)
    low[...] = lows
    high[...] = highs
    for t in range(2):
        out_1[t] = both[rows_ref[t]]
        out_2[t] = both[rows_ref[2 + t]]
    m = 5 * CP
    slots = four_slots(highs, lows)
    spare = jnp.zeros((m, 256 - 5 * hid), F32)
    for which, (stack, outer, edge, grown) in enumerate(
        ((stack_1, outer_1, edge_1, grown_1), (stack_2, outer_2, edge_2, grown_2))
    ):
        mine = slots[hid:] if which == 0 else slots[:hid]
        mine = jnp.concatenate([slid(mine.astype(F32), 2 - k).astype(BF) for k in range(5)], axis=0)
        found = dot_nt(edge[...], mine)
        found = found + correlate_outer(outer, grown, places, flip if which == 1 else None)
        right_side = jnp.concatenate([row_stack(grown, i + 2) for i in range(height)], axis=1)
        found = found + dot_nt(wide(stack, 0, height), right_side)
        found = jnp.concatenate([found, spare], axis=1).astype(WIRE)
        flat[2 * which * m : (2 * which + 1) * m] = found[:, 0:128]
        flat[(2 * which + 1) * m : (2 * which + 2) * m] = found[:, 128:256]
    used = flat.shape[0] - 4 * m
    total = jnp.broadcast_to(jnp.sum(total, axis=1, keepdims=True), (hid, 128))
    coarse = total.astype(WIRE)
    total = jnp.where(lane < 64, coarse, (total - coarse.astype(F32)).astype(WIRE))
    flat[4 * m :] = jnp.concatenate([total, jnp.zeros((used - hid, 128), WIRE)], axis=0)


def second_kernel_body(
    which, rows_ref, both, right, left, rim_1, rim_2, far_1, far_2, weight, base, out, stack, acc,
):
    height = base.shape[1]
    channels = base.shape[0]
    hid = both.shape[1] // 2
    odd = rows_ref[8] == 1
    top = rows_ref[9] == 1
    bottom = rows_ref[10] == 1
    outer = (0, 1, height + 2, height + 3)
    part = slice(which * hid, (which + 1) * hid)
    halo = []
    for side in range(2):
        pick = odd if side == 0 else jnp.logical_not(odd)
        far = [jnp.where(pick, far_1[k, part], far_2[k, part]) for k in range(2)]
        for t in range(2):
            slab = jnp.where(pick, rim_1[t, part], rim_2[t, part])
            halo.append((outer[2 * side + t], slab, far[0], far[1], rows_ref[4 + 2 * side + t]))
    fill_shifted(
        stack, lambda r: both[r, part], lambda: right[part], lambda: left[part], height, halo
    )
    flip = (top, top, bottom, bottom) if which == 1 else None
    conv_rows(acc, stack, weight, CP, height, flip)
    for b in range(height // 16):
        rows = slice(b * 16, (b + 1) * 16)
        block = jnp.swapaxes(acc[b * 16 + 4 : b * 16 + 20], 0, 1)[0:channels]
        out[:, rows, :] = (base[:, rows, :].astype(F32) + block).astype(BF)


def weights_kernel(k_1, k_2, gain, w_1, w_2, w_3, w_4, spread):
    hid, channels = k_1.shape[2:]
    gap = jnp.zeros((hid, CP - channels), F32)
    spread[...] = jnp.broadcast_to(gain[...], (128, hid)).T

    def plane(k, p, q):
        return jnp.concatenate([k[p, q].astype(F32), gap], axis=1)

    for p in range(5):
        rows = slice(p * hid, (p + 1) * hid)
        w_1[rows] = jnp.concatenate([plane(k_1, p, q) for q in range(5)], axis=1).astype(BF)
        w_2[rows] = jnp.concatenate([plane(k_2, 4 - p, 4 - q) for q in range(5)], axis=1).astype(BF)
        rows = slice(p * CP, (p + 1) * CP)
        w_3[rows] = jnp.concatenate([plane(k_2, p, q) for q in range(5)], axis=0).T.astype(BF)
        w_4[rows] = jnp.concatenate([plane(k_1, 4 - p, 4 - q) for q in range(5)], axis=0).T.astype(BF)


def reduce_kernel(factor, rows_ref, got, out):
    devices = got.shape[0]

    def body(i, total):
        return total + got[i].astype(F32)

    total = lax.fori_loop(0, devices, body, jnp.zeros(got.shape[1:], F32), unroll=16)
    mine = (total * factor).astype(BF)
    whole = (total + pltpu.roll(total, 64, 1)) * factor
    coarse = whole.astype(BF)
    fine = (whole - coarse.astype(F32)).astype(BF)
    pair = jnp.where(lanes_of(total.shape) < 64, coarse, fine)
    mine = jnp.where(rows_ref[11] == 1, pair, mine)
    for i in range(devices):
        out[i] = mine


def unpack_kernel(rows, grad_1, grad_2, gain):
    hid, channels = grad_1.shape[2:]
    m = 5 * CP
    for which in range(2):
        at = 2 * which * m
        low = rows[at : at + m].astype(F32).T
        high = rows[at + m : at + 2 * m].astype(F32).T
        both = jnp.concatenate([low, high], axis=0)
        for q in range(5):
            part = both[0 : 5 * hid, q * CP : q * CP + channels]
            for t in range(5):
                piece = part[t * hid : (t + 1) * hid]
                if which == 0:
                    grad_1[4 - t, q] = piece
                else:
                    grad_2[t, 4 - q] = piece
    pair = rows[4 * m : 4 * m + hid].astype(F32).T
    gain[...] = pair[0:1] + pair[64:65]


def call(body, outs, scratch, args, flops, numbers=True, far_in=(), far_out=()):
    near = pl.BlockSpec(memory_space=pltpu.VMEM)
    far = pl.BlockSpec(memory_space=pl.ANY)
    in_specs = [far if i in far_in else near for i in range(len(args))]
    if numbers:
        in_specs[0] = pl.BlockSpec(memory_space=pltpu.SMEM)
    return pl.pallas_call(
        body,
        out_shape=[jax.ShapeDtypeStruct(s, t) for s, t in outs],
        in_specs=in_specs,
        out_specs=[far if i in far_out else near for i in range(len(outs))],
        scratch_shapes=[
            pltpu.SemaphoreType.DMA(s) if t is None else pltpu.VMEM(s, t) for s, t in scratch
        ],
        compiler_params=pltpu.CompilerParams(vmem_limit_bytes=VMEM),
        cost_estimate=pl.CostEstimate(flops=flops, bytes_accessed=1 << 20, transcendentals=0),
    )(*args)


def exchange_columns(low, high):
    count = lax.axis_size("lon")
    up = [(i, (i + 1) % count) for i in range(count)]
    down = [(t, s) for s, t in up]
    right = lax.ppermute(low, "lon", down)
    left = lax.ppermute(high, "lon", up)
    return right, left


def row_routes(lon, lat):
    def at(x, y):
        return (x % lon) * lat + y

    one, two = [], []
    for x in range(lon):
        for y in range(lat):
            one.append((at(x, y), at(x, y + 1 if y % 2 == 0 else y - 1)))
            if y == 0 or y == lat - 1:
                two.append((at(x, y), at(x + lon // 2, y)))
            else:
                two.append((at(x, y), at(x, y - 1 if y % 2 == 0 else y + 1)))
    return one, two


def place_numbers(height, first, last_row, rows):
    lat = lax.axis_index("lat")
    last = lax.axis_size("lat") - 1
    odd = lat % 2
    top = (lat == 0).astype(jnp.int32)
    bottom = (lat == last).astype(jnp.int32)
    h = height
    send_1 = [jnp.where(odd == 1, 0, h - 2), jnp.where(odd == 1, 1, h - 1)]
    send_2 = [
        jnp.where(odd == 1, h - 2 + bottom, top),
        jnp.where(odd == 1, h - 1 - bottom, 1 - top),
    ]
    got = [
        jnp.where(top == 1, 1, h - 2),
        jnp.where(top == 1, 0, h - 1),
        jnp.where(bottom == 1, h - 1, 0),
        jnp.where(bottom == 1, h - 2, 1),
    ]
    begin = (lax.axis_index("lon") * lax.axis_size("lat") + lat) * rows
    is_gain = jnp.logical_and(begin >= first, begin < last_row)
    values = send_1 + send_2 + got + [odd, top, bottom, is_gain]
    return jnp.stack([jnp.asarray(v, jnp.int32) for v in values])


def per_device(field, first_kernel, norm_gain, second_kernel, cotangent):
    channels, height, width = field.shape
    hid = norm_gain.shape[0]
    devices = lax.axis_size("lon") * lax.axis_size("lat")
    rows = -(-(4 * 5 * CP + hid) // (16 * devices)) * 16
    numbers = place_numbers(height, 4 * 5 * CP, 4 * 5 * CP + hid, rows)
    one, two = row_routes(lax.axis_size("lon"), lax.axis_size("lat"))
    us = 10**9

    main, low, high, rim_1, rim_2 = call(
        pack_kernel,
        [
            ((2, height, CP, 128), BF), ((2, CP, 128), BF), ((2, CP, 128), BF),
            ((2, 2, CP, 128), BF), ((2, 2, CP, 128), BF),
        ],
        [],
        (numbers, field, cotangent),
        5 * us,
    )
    right, left = exchange_columns(low, high)
    sides = jnp.stack([right, left], axis=1)
    rim_1, far_1 = lax.ppermute((rim_1, sides), AXES, one)
    rim_2, far_2 = lax.ppermute((rim_2, sides), AXES, two)

    w_1, w_2, w_3, w_4, spread = call(
        weights_kernel,
        [((5 * hid, 5 * CP), BF)] * 2 + [((5 * CP, 5 * hid), BF)] * 2 + [((hid, 128), F32)],
        [],
        (
            jnp.transpose(first_kernel, (2, 3, 0, 1)), jnp.transpose(second_kernel, (2, 3, 1, 0)),
            norm_gain[None],
        ),
        4 * us,
        numbers=False,
    )
    both, low, high, out_1, out_2, flat = call(
        first_kernel_body,
        [
            ((height, 2 * hid, 128), BF), ((2 * hid, 128), BF), ((2 * hid, 128), BF),
            ((2, 2 * hid, 128), BF), ((2, 2 * hid, 128), BF), ((rows * devices, 128), WIRE),
        ],
        [
            ((height, 5 * CP, 128), BF), ((height, 5 * CP, 128), BF),
            ((height + 8, hid, 128), F32), ((height + 8, hid, 128), F32),
            ((height + 8, hid, 128), BF), ((height + 8, hid, 128), BF),
            ((4, 5 * CP, 128), BF), ((4, 5 * CP, 128), BF),
            ((5 * CP, 256), BF), ((5 * CP, 256), BF),
            ((2, hid, 128), F32), ((2, hid, 128), F32),
        ],
        (
            numbers, main, right, left, rim_1, rim_2, far_1, far_2, w_1, w_2, spread,
        ),
        12 * us,
    )

    got = lax.all_to_all(flat.reshape(devices, rows, 128), AXES, 0, 0)
    right, left = exchange_columns(low, high)
    sides = jnp.stack([right, left], axis=0)
    out_1, far_1 = lax.ppermute((out_1, sides), AXES, one)
    out_2, far_2 = lax.ppermute((out_2, sides), AXES, two)
    factor = (height * width * devices) ** -0.5
    (mine,) = call(
        functools.partial(reduce_kernel, factor), [((devices, rows, 128), BF)], [],
        (numbers, got),
        10 * us,
    )
    mine, out_1, out_2, far_1, far_2 = lax.optimization_barrier((mine, out_1, out_2, far_1, far_2))
    summed = lax.all_to_all(mine, AXES, 0, 0).reshape(-1, 128)
    grad_1, grad_2, gain = call(
        unpack_kernel,
        [((5, 5, hid, channels), F32)] * 2 + [((1, hid), F32)],
        [],
        (summed,),
        20 * us,
        numbers=False,
    )
    grad_first = jnp.transpose(grad_1, (2, 3, 0, 1))
    grad_second = jnp.transpose(grad_2, (3, 2, 0, 1))

    results = []
    for which, weight, base in ((0, w_3, field), (1, w_4, cotangent)):
        results += call(
            functools.partial(second_kernel_body, which),
            [(field.shape, BF)],
            [((height + 4, 5 * hid, 128), BF), ((height + 8, CP, 128), F32)],
            (numbers, both, right, left, out_1, out_2, far_1, far_2, weight, base),
            2 * us,
        )
    return results[0], results[1], grad_first, grad_second, gain.reshape(hid)


def solution(mesh):
    placed = (P(None, "lat", "lon"), P(), P(), P(), P(None, "lat", "lon"))
    return jax.shard_map(
        per_device,
        mesh=mesh,
        in_specs=placed,
        out_specs=(P(None, "lat", "lon"), P(None, "lat", "lon"), P(), P(), P()),
        check_vma=False,
    )
```

```python
import functools

import jax
import jax.numpy as jnp
from jax import lax
from jax.experimental import pallas as pl
from jax.experimental.pallas import tpu as pltpu
from jax.sharding import PartitionSpec as P

EPS = 1e-05
BF = jnp.bfloat16
F32 = jnp.float32
AXES = ("lon", "lat")
CP = 80
WIRE = BF
VMEM = 56 * 1024 * 1024


def dot(a, b):
    return jnp.dot(a, b, preferred_element_type=F32)


def dot_nt(a, b):
    return lax.dot_general(a, b, (((1,), (1,)), ((), ())), preferred_element_type=F32)


def lanes_of(shape):
    return lax.broadcasted_iota(jnp.int32, shape, len(shape) - 1)


def edge_columns(read, rows, channels):
    pair = lanes_of((channels, 128)) // 2

    def body(r, found):
        low, high = found
        x = read(r)
        low = jnp.where(pair == r, pltpu.roll(x, 2 * r, 1), low)
        high = jnp.where(pair == r, pltpu.roll(x, lax.rem(2 * r + 2, 128), 1), high)
        return low, high

    zero = jnp.zeros((channels, 128), BF)
    return lax.fori_loop(0, rows, body, (zero, zero), unroll=rows)


def shifted(x, right, left, row):
    lane = lanes_of(x.shape)
    back = lax.rem(128 - 2 * row, 128)
    right = pltpu.roll(right, back, 1)
    left = pltpu.roll(left, lax.rem(254 - 2 * row, 128), 1)
    return [
        pltpu.roll(jnp.where(lane >= 126, left, x), 2, 1),
        pltpu.roll(jnp.where(lane >= 127, left, x), 1, 1),
        x,
        pltpu.roll(jnp.where(lane < 1, right, x), 127, 1),
        pltpu.roll(jnp.where(lane < 2, right, x), 126, 1),
    ]


def store_shifted(out, at, x, right, left, row):
    c = x.shape[0]
    for q, piece in enumerate(shifted(x, right, left, row)):
        out[at, q * c : (q + 1) * c, :] = piece


def fill_shifted(out, read_main, right, left, rows, halo):
    def body(r, carry):
        store_shifted(out, r + 2, read_main(r), right(), left(), r)
        return carry

    lax.fori_loop(0, rows, body, 0, unroll=rows)
    for at, x, far_right, far_left, row in halo:
        store_shifted(out, at, x, far_right, far_left, row)


def wide(ref, start, count):
    return jnp.concatenate([ref[start + t] for t in range(count)], axis=1)


def add_taps(acc, start, y, m, count, flip=None):
    for t in range(count):
        cols = slice(t * 128, (t + 1) * 128)
        for p in range(5):
            part = y[p * m : (p + 1) * m, cols]
            if flip is not None:
                part = jnp.where(flip[t], y[(4 - p) * m : (5 - p) * m, cols], part)
            acc[start[t] + 4 - p] = acc[start[t] + 4 - p] + part


def conv_rows(acc, stack, weight, m, rows, flip=None):
    acc[...] = jnp.zeros(acc.shape, F32)

    y = dot(weight[...], wide(stack, 2, rows))
    add_taps(acc, range(2, rows + 2), y, m, rows)
    outer = (0, 1, rows + 2, rows + 3)
    y = dot(weight[...], jnp.concatenate([stack[i] for i in outer], axis=1))
    add_taps(acc, outer, y, m, 4, flip)


def row_stack(ref, i):
    return ref[pl.ds(i, 5)].reshape(5 * ref.shape[1], 128)


def correlate_outer(outer, grown, places, flip=None):
    pieces = []
    for t, i in enumerate(places):
        piece = row_stack(grown, i)
        if flip is not None:
            turned = jnp.concatenate([grown[i + 4 - m] for m in range(5)], axis=0)
            piece = jnp.where(flip[t], turned, piece)
        pieces.append(piece)
    return dot_nt(wide(outer, 0, 4), jnp.concatenate(pieces, axis=1))


def shifted_alone(x):
    lane = lanes_of(x.shape)
    zero = jnp.zeros_like(x)
    return [
        jnp.where(lane < 2, zero, pltpu.roll(x, 2, 1)),
        jnp.where(lane < 1, zero, pltpu.roll(x, 1, 1)),
        x,
        jnp.where(lane >= 127, zero, pltpu.roll(x, 127, 1)),
        jnp.where(lane >= 126, zero, pltpu.roll(x, 126, 1)),
    ]


def four_slots(high, low):
    source = lax.broadcasted_iota(jnp.int32, (256, 256), 0)
    target = lax.broadcasted_iota(jnp.int32, (256, 256), 1)
    side = (source >= 128).astype(jnp.int32)
    place = 4 * ((source - 128 * side) // 2) + source % 2 + 2 * side
    route = (target == place).astype(F32).astype(BF)
    return dot(jnp.concatenate([high, low], axis=1), route).astype(BF)


def edge_stack(right, left):
    c = right.shape[0]
    odd = lanes_of(right.shape) % 2 == 1
    zero = jnp.zeros_like(right)
    high = [zero, zero, zero, jnp.where(odd, pltpu.roll(right, 1, 1), zero), right]
    low = [left, jnp.where(odd, zero, pltpu.roll(left, 127, 1)), zero, zero, zero]
    return four_slots(jnp.concatenate(high, axis=0), jnp.concatenate(low, axis=0))


def slid(x, rows):
    by = 4 * rows
    if by == 0:
        return x
    lane = lanes_of(x.shape)
    inside = lane >= by if by > 0 else lane < 256 + by
    return jnp.where(inside, pltpu.roll(x, by % 256, 1), jnp.zeros_like(x))


def conv_alone(main, which, stack, weight, acc):
    height = main.shape[1]

    def body(r, carry):
        for q, piece in enumerate(shifted_alone(main[which, r])):
            stack[r, q * CP : (q + 1) * CP] = piece
        return carry

    lax.fori_loop(0, height, body, 0, unroll=8)
    acc[...] = jnp.zeros(acc.shape, F32)
    y = dot(weight[...], wide(stack, 0, height))
    add_taps(acc, range(2, height + 2), y, acc.shape[1], height)


def pack_kernel(rows_ref, field, cot, main, low, high, rim_1, rim_2):
    height = field.shape[1]
    lost = CP - field.shape[0]
    for which, source in enumerate((field, cot)):
        for b in range(height // 16):
            block = source[:, b * 16 : (b + 1) * 16, :].astype(F32)
            block = jnp.concatenate([block, jnp.zeros((lost, 16, 128), F32)], axis=0)
            main[which, b * 16 : (b + 1) * 16] = jnp.swapaxes(block, 0, 1).astype(BF)
        low[which], high[which] = edge_columns(lambda r: main[which, r], height, CP)
        for t in range(2):
            rim_1[which, t] = main[which, rows_ref[t]]
            rim_2[which, t] = main[which, rows_ref[2 + t]]


def halo_slabs(rows_ref, odd, got_1, got_2, which):
    got = []
    for side in range(2):
        upper = side == 0
        pick = odd if upper else jnp.logical_not(odd)
        far = [jnp.where(pick, got_1[which, 2 + k], got_2[which, 2 + k]) for k in range(2)]
        for t in range(2):
            slab = jnp.where(pick, got_1[which, t], got_2[which, t])
            got.append((slab, far[0], far[1], rows_ref[4 + 2 * side + t]))
    return got


def first_kernel_body(
    rows_ref, main, right, left, got_1, got_2, w_1, w_2, gain,
    both, low, high, out_1, out_2, flat,
    stack_1, stack_2, acc_1, acc_2, grown_1, grown_2, outer_1, outer_2, edge_1, edge_2, z_1, z_2,
):
    height, _, _ = both.shape
    hid = gain.shape[0]
    odd = rows_ref[8] == 1
    top = rows_ref[9] == 1
    bottom = rows_ref[10] == 1
    flip = (top, top, bottom, bottom)
    places = (0, 1, height + 2, height + 3)
    for grown in (grown_1, grown_2):
        grown[0:4] = jnp.zeros((4, hid, 128), BF)
        grown[height + 4 : height + 8] = jnp.zeros((4, hid, 128), BF)
    weights = (w_1, w_2)
    for which, (outer, edge, z) in enumerate(((outer_1, edge_1, z_1), (outer_2, edge_2, z_2))):
        halo = halo_slabs(rows_ref, odd, got_1, got_2, which)
        for t in range(4):
            store_shifted(outer, t, *halo[t])
        edge[...] = edge_stack(right[which], left[which])
        y = dot(weights[which][...], edge[...])
        found = sum(slid(y[p * hid : (p + 1) * hid], 2 - p) for p in range(5))
        z[0] = found[:, 0:128]
        z[1] = found[:, 128:256]
    conv_alone(main, 0, stack_1, w_1, acc_1)
    conv_alone(main, 1, stack_2, w_2, acc_2)
    for which, (outer, acc) in enumerate(((outer_1, acc_1), (outer_2, acc_2))):
        y = dot(weights[which][...], wide(outer, 0, 4))
        add_taps(acc, places, y, hid, 4, flip if which == 1 else None)
    spread = gain[...]
    lane = lanes_of((hid, 128))
    side = jnp.logical_or(lane < 2, lane >= 126)

    def cells(r, total):
        turn = lax.rem(382 - 4 * r, 128)

        def with_edges(acc, z):
            return acc[r + 4] + jnp.where(side, pltpu.roll(z[r // 32], turn, 1), 0.0)

        pre = with_edges(acc_1, z_1)
        grad_act = with_edges(acc_2, z_2)
        scale = lax.rsqrt(jnp.mean(pre * pre, axis=0, keepdims=True) + EPS)
        unit = pre * scale
        normed = unit * spread
        sig = 1.0 / (1.0 + jnp.exp(-normed))
        active = (normed * sig).astype(BF)
        grad_normed = grad_act * sig * (1.0 + normed * (1.0 - sig))
        g2 = grad_normed * spread
        mean = jnp.mean(g2 * pre, axis=0, keepdims=True)
        grad_pre = (scale * g2 - pre * (scale * scale * scale * mean)).astype(BF)
        grown_1[r + 4] = grad_pre
        grown_2[r + 4] = active
        both[r, 0:hid] = active
        both[r, hid : 2 * hid] = grad_pre
        return total + grad_normed * unit

    total = lax.fori_loop(0, height, cells, jnp.zeros((hid, 128), F32), unroll=16)
    lows, highs = edge_columns(lambda r: both[r], height, 2 * hid)
    low[...] = lows
    high[...] = highs
    for t in range(2):
        out_1[t] = both[rows_ref[t]]
        out_2[t] = both[rows_ref[2 + t]]
    m = 5 * CP
    slots = four_slots(highs, lows)
    spare = jnp.zeros((m, 256 - 5 * hid), F32)
    for which, (stack, outer, edge, grown) in enumerate(
        ((stack_1, outer_1, edge_1, grown_1), (stack_2, outer_2, edge_2, grown_2))
    ):
        mine = slots[hid:] if which == 0 else slots[:hid]
        mine = jnp.concatenate([slid(mine.astype(F32), 2 - k).astype(BF) for k in range(5)], axis=0)
        found = dot_nt(edge[...], mine)
        found = found + correlate_outer(outer, grown, places, flip if which == 1 else None)
        right_side = jnp.concatenate([row_stack(grown, i + 2) for i in range(height)], axis=1)
        found = found + dot_nt(wide(stack, 0, height), right_side)
        found = jnp.concatenate([found, spare], axis=1).astype(WIRE)
        flat[2 * which * m : (2 * which + 1) * m] = found[:, 0:128]
        flat[(2 * which + 1) * m : (2 * which + 2) * m] = found[:, 128:256]
    used = flat.shape[0] - 4 * m
    total = jnp.broadcast_to(jnp.sum(total, axis=1, keepdims=True), (hid, 128))
    coarse = total.astype(WIRE)
    total = jnp.where(lane < 64, coarse, (total - coarse.astype(F32)).astype(WIRE))
    flat[4 * m :] = jnp.concatenate([total, jnp.zeros((used - hid, 128), WIRE)], axis=0)


def second_kernel_body(
    which, rows_ref, both, right, left, got_1, got_2, weight, base, out, stack, acc,
):
    height = base.shape[1]
    channels = base.shape[0]
    hid = both.shape[1] // 2
    odd = rows_ref[8] == 1
    top = rows_ref[9] == 1
    bottom = rows_ref[10] == 1
    outer = (0, 1, height + 2, height + 3)
    part = slice(which * hid, (which + 1) * hid)
    halo = []
    for side in range(2):
        pick = odd if side == 0 else jnp.logical_not(odd)
        far = [jnp.where(pick, got_1[2 + k, part], got_2[2 + k, part]) for k in range(2)]
        for t in range(2):
            slab = jnp.where(pick, got_1[t, part], got_2[t, part])
            halo.append((outer[2 * side + t], slab, far[0], far[1], rows_ref[4 + 2 * side + t]))
    fill_shifted(
        stack, lambda r: both[r, part], lambda: right[part], lambda: left[part], height, halo
    )
    flip = (top, top, bottom, bottom) if which == 1 else None
    conv_rows(acc, stack, weight, CP, height, flip)
    for b in range(height // 16):
        rows = slice(b * 16, (b + 1) * 16)
        block = jnp.swapaxes(acc[b * 16 + 4 : b * 16 + 20], 0, 1)[0:channels]
        out[:, rows, :] = (base[:, rows, :].astype(F32) + block).astype(BF)


def weights_kernel(k_1, k_2, gain, w_1, w_2, w_3, w_4, spread):
    hid, channels = k_1.shape[2:]
    gap = jnp.zeros((hid, CP - channels), F32)
    spread[...] = jnp.broadcast_to(gain[...], (128, hid)).T

    def plane(k, p, q):
        return jnp.concatenate([k[p, q].astype(F32), gap], axis=1)

    for p in range(5):
        rows = slice(p * hid, (p + 1) * hid)
        w_1[rows] = jnp.concatenate([plane(k_1, p, q) for q in range(5)], axis=1).astype(BF)
        w_2[rows] = jnp.concatenate([plane(k_2, 4 - p, 4 - q) for q in range(5)], axis=1).astype(BF)
        rows = slice(p * CP, (p + 1) * CP)
        w_3[rows] = jnp.concatenate([plane(k_2, p, q) for q in range(5)], axis=0).T.astype(BF)
        w_4[rows] = jnp.concatenate([plane(k_1, 4 - p, 4 - q) for q in range(5)], axis=0).T.astype(BF)


def reduce_kernel(factor, rows_ref, got, out):
    devices = got.shape[0]

    def body(i, total):
        return total + got[i].astype(F32)

    total = lax.fori_loop(0, devices, body, jnp.zeros(got.shape[1:], F32), unroll=16)
    mine = (total * factor).astype(BF)
    whole = (total + pltpu.roll(total, 64, 1)) * factor
    coarse = whole.astype(BF)
    fine = (whole - coarse.astype(F32)).astype(BF)
    pair = jnp.where(lanes_of(total.shape) < 64, coarse, fine)
    mine = jnp.where(rows_ref[11] == 1, pair, mine)
    for i in range(devices):
        out[i] = mine


def unpack_kernel(rows, grad_1, grad_2, gain):
    hid, channels = grad_1.shape[2:]
    m = 5 * CP
    for which in range(2):
        at = 2 * which * m
        low = rows[at : at + m].astype(F32).T
        high = rows[at + m : at + 2 * m].astype(F32).T
        both = jnp.concatenate([low, high], axis=0)
        for q in range(5):
            part = both[0 : 5 * hid, q * CP : q * CP + channels]
            for t in range(5):
                piece = part[t * hid : (t + 1) * hid]
                if which == 0:
                    grad_1[4 - t, q] = piece
                else:
                    grad_2[t, 4 - q] = piece
    pair = rows[4 * m : 4 * m + hid].astype(F32).T
    gain[...] = pair[0:1] + pair[64:65]


def call(body, outs, scratch, args, flops, numbers=True, far_in=(), far_out=()):
    near = pl.BlockSpec(memory_space=pltpu.VMEM)
    far = pl.BlockSpec(memory_space=pl.ANY)
    in_specs = [far if i in far_in else near for i in range(len(args))]
    if numbers:
        in_specs[0] = pl.BlockSpec(memory_space=pltpu.SMEM)
    return pl.pallas_call(
        body,
        out_shape=[jax.ShapeDtypeStruct(s, t) for s, t in outs],
        in_specs=in_specs,
        out_specs=[far if i in far_out else near for i in range(len(outs))],
        scratch_shapes=[
            pltpu.SemaphoreType.DMA(s) if t is None else pltpu.VMEM(s, t) for s, t in scratch
        ],
        compiler_params=pltpu.CompilerParams(vmem_limit_bytes=VMEM),
        cost_estimate=pl.CostEstimate(flops=flops, bytes_accessed=1 << 20, transcendentals=0),
    )(*args)


def exchange_columns(low, high):
    count = lax.axis_size("lon")
    up = [(i, (i + 1) % count) for i in range(count)]
    down = [(t, s) for s, t in up]
    right = lax.ppermute(low, "lon", down)
    left = lax.ppermute(high, "lon", up)
    return right, left


def row_routes(lon, lat):
    def at(x, y):
        return (x % lon) * lat + y

    one, two = [], []
    for x in range(lon):
        for y in range(lat):
            one.append((at(x, y), at(x, y + 1 if y % 2 == 0 else y - 1)))
            if y == 0 or y == lat - 1:
                two.append((at(x, y), at(x + lon // 2, y)))
            else:
                two.append((at(x, y), at(x, y - 1 if y % 2 == 0 else y + 1)))
    return one, two


def place_numbers(height, first, last_row, rows):
    lat = lax.axis_index("lat")
    last = lax.axis_size("lat") - 1
    odd = lat % 2
    top = (lat == 0).astype(jnp.int32)
    bottom = (lat == last).astype(jnp.int32)
    h = height
    send_1 = [jnp.where(odd == 1, 0, h - 2), jnp.where(odd == 1, 1, h - 1)]
    send_2 = [
        jnp.where(odd == 1, h - 2 + bottom, top),
        jnp.where(odd == 1, h - 1 - bottom, 1 - top),
    ]
    got = [
        jnp.where(top == 1, 1, h - 2),
        jnp.where(top == 1, 0, h - 1),
        jnp.where(bottom == 1, h - 1, 0),
        jnp.where(bottom == 1, h - 2, 1),
    ]
    begin = (lax.axis_index("lon") * lax.axis_size("lat") + lat) * rows
    is_gain = jnp.logical_and(begin >= first, begin < last_row)
    values = send_1 + send_2 + got + [odd, top, bottom, is_gain]
    return jnp.stack([jnp.asarray(v, jnp.int32) for v in values])


def per_device(field, first_kernel, norm_gain, second_kernel, cotangent):
    channels, height, width = field.shape
    hid = norm_gain.shape[0]
    devices = lax.axis_size("lon") * lax.axis_size("lat")
    rows = -(-(4 * 5 * CP + hid) // (16 * devices)) * 16
    numbers = place_numbers(height, 4 * 5 * CP, 4 * 5 * CP + hid, rows)
    one, two = row_routes(lax.axis_size("lon"), lax.axis_size("lat"))
    us = 10**9

    main, low, high, rim_1, rim_2 = call(
        pack_kernel,
        [
            ((2, height, CP, 128), BF), ((2, CP, 128), BF), ((2, CP, 128), BF),
            ((2, 2, CP, 128), BF), ((2, 2, CP, 128), BF),
        ],
        [],
        (numbers, field, cotangent),
        5 * us,
    )
    right, left = exchange_columns(low, high)
    sides = jnp.stack([right, left], axis=1)
    got_1 = lax.ppermute(jnp.concatenate([rim_1, sides], axis=1), AXES, one)
    got_2 = lax.ppermute(jnp.concatenate([rim_2, sides], axis=1), AXES, two)

    w_1, w_2, w_3, w_4, spread = call(
        weights_kernel,
        [((5 * hid, 5 * CP), BF)] * 2 + [((5 * CP, 5 * hid), BF)] * 2 + [((hid, 128), F32)],
        [],
        (
            jnp.transpose(first_kernel, (2, 3, 0, 1)), jnp.transpose(second_kernel, (2, 3, 1, 0)),
            norm_gain[None],
        ),
        4 * us,
        numbers=False,
    )
    both, low, high, out_1, out_2, flat = call(
        first_kernel_body,
        [
            ((height, 2 * hid, 128), BF), ((2 * hid, 128), BF), ((2 * hid, 128), BF),
            ((2, 2 * hid, 128), BF), ((2, 2 * hid, 128), BF), ((rows * devices, 128), WIRE),
        ],
        [
            ((height, 5 * CP, 128), BF), ((height, 5 * CP, 128), BF),
            ((height + 8, hid, 128), F32), ((height + 8, hid, 128), F32),
            ((height + 8, hid, 128), BF), ((height + 8, hid, 128), BF),
            ((4, 5 * CP, 128), BF), ((4, 5 * CP, 128), BF),
            ((5 * CP, 256), BF), ((5 * CP, 256), BF),
            ((2, hid, 128), F32), ((2, hid, 128), F32),
        ],
        (
            numbers, main, right, left, got_1, got_2, w_1, w_2, spread,
        ),
        12 * us,
    )

    got = lax.all_to_all(flat.reshape(devices, rows, 128), AXES, 0, 0)
    right, left = exchange_columns(low, high)
    sides = jnp.stack([right, left], axis=0)
    out_1 = lax.ppermute(jnp.concatenate([out_1, sides], axis=0), AXES, one)
    out_2 = lax.ppermute(jnp.concatenate([out_2, sides], axis=0), AXES, two)
    factor = (height * width * devices) ** -0.5
    (mine,) = call(
        functools.partial(reduce_kernel, factor), [((devices, rows, 128), BF)], [],
        (numbers, got),
        10 * us,
    )
    mine, out_1, out_2 = lax.optimization_barrier((mine, out_1, out_2))
    summed = lax.all_to_all(mine, AXES, 0, 0).reshape(-1, 128)
    grad_1, grad_2, gain = call(
        unpack_kernel,
        [((5, 5, hid, channels), F32)] * 2 + [((1, hid), F32)],
        [],
        (summed,),
        20 * us,
        numbers=False,
    )
    grad_first = jnp.transpose(grad_1, (2, 3, 0, 1))
    grad_second = jnp.transpose(grad_2, (3, 2, 0, 1))

    results = []
    for which, weight, base in ((0, w_3, field), (1, w_4, cotangent)):
        results += call(
            functools.partial(second_kernel_body, which),
            [(field.shape, BF)],
            [((height + 4, 5 * hid, 128), BF), ((height + 8, CP, 128), F32)],
            (numbers, both, right, left, out_1, out_2, weight, base),
            2 * us,
        )
    return results[0], results[1], grad_first, grad_second, gain.reshape(hid)


def solution(mesh):
    placed = (P(None, "lat", "lon"), P(), P(), P(), P(None, "lat", "lon"))
    return jax.shard_map(
        per_device,
        mesh=mesh,
        in_specs=placed,
        out_specs=(P(None, "lat", "lon"), P(None, "lat", "lon"), P(), P(), P()),
        check_vma=False,
    )
```

```python
import functools

import jax
import jax.numpy as jnp
from jax import lax
from jax.experimental import pallas as pl
from jax.experimental.pallas import tpu as pltpu
from jax.sharding import PartitionSpec as P

EPS = 1e-05
BF = jnp.bfloat16
F32 = jnp.float32
AXES = ("lon", "lat")
CP = 80
WIRE = BF


def dot(a, b):
    return jnp.dot(a, b, preferred_element_type=F32)


def dot_nt(a, b):
    return lax.dot_general(a, b, (((1,), (1,)), ((), ())), preferred_element_type=F32)


def lanes_of(shape):
    return lax.broadcasted_iota(jnp.int32, shape, len(shape) - 1)


def edge_columns(read, rows, channels):
    pair = lanes_of((channels, 128)) // 2

    def body(r, found):
        low, high = found
        x = read(r)
        low = jnp.where(pair == r, pltpu.roll(x, 2 * r, 1), low)
        high = jnp.where(pair == r, pltpu.roll(x, lax.rem(2 * r + 2, 128), 1), high)
        return low, high

    zero = jnp.zeros((channels, 128), BF)
    return lax.fori_loop(0, rows, body, (zero, zero), unroll=rows)


def shifted(x, right, left, row):
    lane = lanes_of(x.shape)
    back = lax.rem(128 - 2 * row, 128)
    right = pltpu.roll(right, back, 1)
    left = pltpu.roll(left, lax.rem(254 - 2 * row, 128), 1)
    return [
        pltpu.roll(jnp.where(lane >= 126, left, x), 2, 1),
        pltpu.roll(jnp.where(lane >= 127, left, x), 1, 1),
        x,
        pltpu.roll(jnp.where(lane < 1, right, x), 127, 1),
        pltpu.roll(jnp.where(lane < 2, right, x), 126, 1),
    ]


def store_shifted(out, at, x, right, left, row):
    c = x.shape[0]
    for q, piece in enumerate(shifted(x, right, left, row)):
        out[at, q * c : (q + 1) * c, :] = piece


def fill_shifted(out, read_main, right, left, rows, halo):
    def body(r, carry):
        store_shifted(out, r + 2, read_main(r), right(), left(), r)
        return carry

    lax.fori_loop(0, rows, body, 0, unroll=rows)
    for at, x, far_right, far_left, row in halo:
        store_shifted(out, at, x, far_right, far_left, row)


def wide(ref, start, count):
    return jnp.concatenate([ref[start + t] for t in range(count)], axis=1)


def add_taps(acc, start, y, m, count, flip=None):
    for t in range(count):
        cols = slice(t * 128, (t + 1) * 128)
        for p in range(5):
            part = y[p * m : (p + 1) * m, cols]
            if flip is not None:
                part = jnp.where(flip[t], y[(4 - p) * m : (5 - p) * m, cols], part)
            acc[start[t] + 4 - p] = acc[start[t] + 4 - p] + part


def store_taps(acc, y, m, rows):
    for k in range(rows + 8):
        parts = [
            y[p * m : (p + 1) * m, (k - 6 + p) * 128 : (k - 5 + p) * 128]
            for p in range(5)
            if 0 <= k - 6 + p < rows
        ]
        acc[k] = sum(parts[1:], parts[0]) if parts else jnp.zeros(acc.shape[1:], F32)


def conv_rows(acc, stack, weight, m, rows, flip=None):
    y = dot(weight[...], wide(stack, 2, rows))
    store_taps(acc, y, m, rows)
    outer = (0, 1, rows + 2, rows + 3)
    y = dot(weight[...], jnp.concatenate([stack[i] for i in outer], axis=1))
    add_taps(acc, outer, y, m, 4, flip)


def row_stack(ref, i):
    return ref[pl.ds(i, 5)].reshape(5 * ref.shape[1], 128)


def correlate_outer(outer, grown, places, flip=None):
    pieces = []
    for t, i in enumerate(places):
        piece = row_stack(grown, i)
        if flip is not None:
            turned = jnp.concatenate([grown[i + 4 - m] for m in range(5)], axis=0)
            piece = jnp.where(flip[t], turned, piece)
        pieces.append(piece)
    return dot_nt(wide(outer, 0, 4), jnp.concatenate(pieces, axis=1))


def shifted_alone(x):
    lane = lanes_of(x.shape)
    zero = jnp.zeros_like(x)
    return [
        jnp.where(lane < 2, zero, pltpu.roll(x, 2, 1)),
        jnp.where(lane < 1, zero, pltpu.roll(x, 1, 1)),
        x,
        jnp.where(lane >= 127, zero, pltpu.roll(x, 127, 1)),
        jnp.where(lane >= 126, zero, pltpu.roll(x, 126, 1)),
    ]


def four_slots(high, low):
    source = lax.broadcasted_iota(jnp.int32, (256, 256), 0)
    target = lax.broadcasted_iota(jnp.int32, (256, 256), 1)
    side = (source >= 128).astype(jnp.int32)
    place = 4 * ((source - 128 * side) // 2) + source % 2 + 2 * side
    route = (target == place).astype(F32).astype(BF)
    return dot(jnp.concatenate([high, low], axis=1), route).astype(BF)


def edge_stack(right, left):
    c = right.shape[0]
    odd = lanes_of(right.shape) % 2 == 1
    zero = jnp.zeros_like(right)
    high = [zero, zero, zero, jnp.where(odd, pltpu.roll(right, 1, 1), zero), right]
    low = [left, jnp.where(odd, zero, pltpu.roll(left, 127, 1)), zero, zero, zero]
    return four_slots(jnp.concatenate(high, axis=0), jnp.concatenate(low, axis=0))


def slid(x, rows):
    by = 4 * rows
    if by == 0:
        return x
    lane = lanes_of(x.shape)
    inside = lane >= by if by > 0 else lane < 256 + by
    return jnp.where(inside, pltpu.roll(x, by % 256, 1), jnp.zeros_like(x))


def conv_alone(main, which, stack, weight, acc):
    height = main.shape[1]

    def body(r, carry):
        for q, piece in enumerate(shifted_alone(main[which, r])):
            stack[r, q * CP : (q + 1) * CP] = piece
        return carry

    lax.fori_loop(0, height, body, 0, unroll=8)
    y = dot(weight[...], wide(stack, 0, height))
    store_taps(acc, y, acc.shape[1], height)


def pack_kernel(rows_ref, field, cot, main, low, high, rim_1, rim_2):
    height = field.shape[1]
    lost = CP - field.shape[0]
    for which, source in enumerate((field, cot)):
        for b in range(height // 16):
            block = source[:, b * 16 : (b + 1) * 16, :].astype(F32)
            block = jnp.concatenate([block, jnp.zeros((lost, 16, 128), F32)], axis=0)
            main[which, b * 16 : (b + 1) * 16] = jnp.swapaxes(block, 0, 1).astype(BF)
        low[which], high[which] = edge_columns(lambda r: main[which, r], height, CP)
        for t in range(2):
            rim_1[which, t] = main[which, rows_ref[t]]
            rim_2[which, t] = main[which, rows_ref[2 + t]]


def halo_slabs(rows_ref, odd, rim_1, rim_2, far_1, far_2, which):
    got = []
    for side in range(2):
        upper = side == 0
        pick = odd if upper else jnp.logical_not(odd)
        far = [jnp.where(pick, far_1[which, k], far_2[which, k]) for k in range(2)]
        for t in range(2):
            slab = jnp.where(pick, rim_1[which, t], rim_2[which, t])
            got.append((slab, far[0], far[1], rows_ref[4 + 2 * side + t]))
    return got


def first_kernel_body(
    rows_ref, main, right, left, rim_1, rim_2, far_1, far_2, w_1, w_2, gain,
    both, low, high, out_1, out_2, flat,
    stack_1, stack_2, acc_1, acc_2, grown_1, grown_2, outer_1, outer_2, edge_1, edge_2, z_1, z_2,
):
    height, _, _ = both.shape
    hid = gain.shape[0]
    odd = rows_ref[8] == 1
    top = rows_ref[9] == 1
    bottom = rows_ref[10] == 1
    flip = (top, top, bottom, bottom)
    places = (0, 1, height + 2, height + 3)
    for grown in (grown_1, grown_2):
        grown[0:4] = jnp.zeros((4, hid, 128), BF)
        grown[height + 4 : height + 8] = jnp.zeros((4, hid, 128), BF)
    weights = (w_1, w_2)
    for which, (outer, edge, z) in enumerate(((outer_1, edge_1, z_1), (outer_2, edge_2, z_2))):
        halo = halo_slabs(rows_ref, odd, rim_1, rim_2, far_1, far_2, which)
        for t in range(4):
            store_shifted(outer, t, *halo[t])
        edge[...] = edge_stack(right[which], left[which])
        y = dot(weights[which][...], edge[...])
        found = sum(slid(y[p * hid : (p + 1) * hid], 2 - p) for p in range(5))
        z[0] = found[:, 0:128]
        z[1] = found[:, 128:256]
    conv_alone(main, 0, stack_1, w_1, acc_1)
    conv_alone(main, 1, stack_2, w_2, acc_2)
    for which, (outer, acc) in enumerate(((outer_1, acc_1), (outer_2, acc_2))):
        y = dot(weights[which][...], wide(outer, 0, 4))
        add_taps(acc, places, y, hid, 4, flip if which == 1 else None)
    spread = gain[...]
    lane = lanes_of((hid, 128))
    side = jnp.logical_or(lane < 2, lane >= 126)

    def cells(r, total):
        turn = lax.rem(382 - 4 * r, 128)

        def with_edges(acc, z):
            return acc[r + 4] + jnp.where(side, pltpu.roll(z[r // 32], turn, 1), 0.0)

        pre = with_edges(acc_1, z_1)
        grad_act = with_edges(acc_2, z_2)
        scale = lax.rsqrt(jnp.mean(pre * pre, axis=0, keepdims=True) + EPS)
        unit = pre * scale
        normed = unit * spread
        sig = 1.0 / (1.0 + jnp.exp(-normed))
        active = (normed * sig).astype(BF)
        grad_normed = grad_act * sig * (1.0 + normed * (1.0 - sig))
        g2 = grad_normed * spread
        mean = jnp.mean(g2 * pre, axis=0, keepdims=True)
        grad_pre = (scale * g2 - pre * (scale * scale * scale * mean)).astype(BF)
        grown_1[r + 4] = grad_pre
        grown_2[r + 4] = active
        both[r, 0:hid] = active
        both[r, hid : 2 * hid] = grad_pre
        return total + grad_normed * unit

    total = lax.fori_loop(0, height, cells, jnp.zeros((hid, 128), F32), unroll=16)
    lows, highs = edge_columns(lambda r: both[r], height, 2 * hid)
    low[...] = lows
    high[...] = highs
    for t in range(2):
        out_1[t] = both[rows_ref[t]]
        out_2[t] = both[rows_ref[2 + t]]
    m = 5 * CP
    slots = four_slots(highs, lows)
    spare = jnp.zeros((m, 256 - 5 * hid), F32)
    for which, (stack, outer, edge, grown) in enumerate(
        ((stack_1, outer_1, edge_1, grown_1), (stack_2, outer_2, edge_2, grown_2))
    ):
        mine = slots[hid:] if which == 0 else slots[:hid]
        mine = jnp.concatenate([slid(mine.astype(F32), 2 - k).astype(BF) for k in range(5)], axis=0)
        found = dot_nt(edge[...], mine)
        found = found + correlate_outer(outer, grown, places, flip if which == 1 else None)
        right_side = jnp.concatenate([row_stack(grown, i + 2) for i in range(height)], axis=1)
        found = found + dot_nt(wide(stack, 0, height), right_side)
        found = jnp.concatenate([found, spare], axis=1).astype(WIRE)
        flat[2 * which * m : (2 * which + 1) * m] = found[:, 0:128]
        flat[(2 * which + 1) * m : (2 * which + 2) * m] = found[:, 128:256]
    used = flat.shape[0] - 4 * m
    total = jnp.broadcast_to(jnp.sum(total, axis=1, keepdims=True), (hid, 128))
    coarse = total.astype(WIRE)
    total = jnp.where(lane < 64, coarse, (total - coarse.astype(F32)).astype(WIRE))
    flat[4 * m :] = jnp.concatenate([total, jnp.zeros((used - hid, 128), WIRE)], axis=0)


def second_kernel_body(
    which, rows_ref, both, right, left, rim_1, rim_2, far_1, far_2, weight, base, out, stack, acc,
):
    height = base.shape[1]
    channels = base.shape[0]
    hid = both.shape[1] // 2
    odd = rows_ref[8] == 1
    top = rows_ref[9] == 1
    bottom = rows_ref[10] == 1
    outer = (0, 1, height + 2, height + 3)
    part = slice(which * hid, (which + 1) * hid)
    halo = []
    for side in range(2):
        pick = odd if side == 0 else jnp.logical_not(odd)
        far = [jnp.where(pick, far_1[k, part], far_2[k, part]) for k in range(2)]
        for t in range(2):
            slab = jnp.where(pick, rim_1[t, part], rim_2[t, part])
            halo.append((outer[2 * side + t], slab, far[0], far[1], rows_ref[4 + 2 * side + t]))
    fill_shifted(
        stack, lambda r: both[r, part], lambda: right[part], lambda: left[part], height, halo
    )
    flip = (top, top, bottom, bottom) if which == 1 else None
    conv_rows(acc, stack, weight, CP, height, flip)
    for b in range(height // 16):
        rows = slice(b * 16, (b + 1) * 16)
        block = jnp.swapaxes(acc[b * 16 + 4 : b * 16 + 20], 0, 1)[0:channels]
        out[:, rows, :] = (base[:, rows, :].astype(F32) + block).astype(BF)


def weights_kernel(k_1, k_2, gain, w_1, w_2, w_3, w_4, spread):
    hid, channels = k_1.shape[2:]
    gap = jnp.zeros((hid, CP - channels), F32)
    spread[...] = jnp.broadcast_to(gain[...], (128, hid)).T

    def plane(k, p, q):
        return jnp.concatenate([k[p, q].astype(F32), gap], axis=1)

    for p in range(5):
        rows = slice(p * hid, (p + 1) * hid)
        w_1[rows] = jnp.concatenate([plane(k_1, p, q) for q in range(5)], axis=1).astype(BF)
        w_2[rows] = jnp.concatenate([plane(k_2, 4 - p, 4 - q) for q in range(5)], axis=1).astype(BF)
        rows = slice(p * CP, (p + 1) * CP)
        w_3[rows] = jnp.concatenate([plane(k_2, p, q) for q in range(5)], axis=0).T.astype(BF)
        w_4[rows] = jnp.concatenate([plane(k_1, 4 - p, 4 - q) for q in range(5)], axis=0).T.astype(BF)


def reduce_kernel(factor, rows_ref, got, out):
    devices = got.shape[0]

    def body(i, total):
        return total + got[i].astype(F32)

    total = lax.fori_loop(0, devices, body, jnp.zeros(got.shape[1:], F32), unroll=16)
    mine = (total * factor).astype(BF)
    whole = (total + pltpu.roll(total, 64, 1)) * factor
    coarse = whole.astype(BF)
    fine = (whole - coarse.astype(F32)).astype(BF)
    pair = jnp.where(lanes_of(total.shape) < 64, coarse, fine)
    mine = jnp.where(rows_ref[11] == 1, pair, mine)
    for i in range(devices):
        out[i] = mine


def unpack_kernel(rows, grad_1, grad_2, gain):
    hid, channels = grad_1.shape[2:]
    m = 5 * CP
    for which in range(2):
        at = 2 * which * m
        low = rows[at : at + m].astype(F32).T
        high = rows[at + m : at + 2 * m].astype(F32).T
        both = jnp.concatenate([low, high], axis=0)
        for q in range(5):
            part = both[0 : 5 * hid, q * CP : q * CP + channels]
            for t in range(5):
                piece = part[t * hid : (t + 1) * hid]
                if which == 0:
                    grad_1[4 - t, q] = piece
                else:
                    grad_2[t, 4 - q] = piece
    pair = rows[4 * m : 4 * m + hid].astype(F32).T
    gain[...] = pair[0:1] + pair[64:65]


def call(body, outs, scratch, args, flops, mib, numbers=True):
    near = pl.BlockSpec(memory_space=pltpu.VMEM)
    in_specs = [near] * len(args)
    if numbers:
        in_specs[0] = pl.BlockSpec(memory_space=pltpu.SMEM)
    return pl.pallas_call(
        body,
        out_shape=[jax.ShapeDtypeStruct(s, t) for s, t in outs],
        in_specs=in_specs,
        out_specs=[near] * len(outs),
        scratch_shapes=[pltpu.VMEM(s, t) for s, t in scratch],
        compiler_params=pltpu.CompilerParams(vmem_limit_bytes=mib << 20),
        cost_estimate=pl.CostEstimate(flops=flops, bytes_accessed=1 << 20, transcendentals=0),
    )(*args)


def exchange_columns(low, high):
    count = lax.axis_size("lon")
    up = [(i, (i + 1) % count) for i in range(count)]
    down = [(t, s) for s, t in up]
    right = lax.ppermute(low, "lon", down)
    left = lax.ppermute(high, "lon", up)
    return right, left


def row_routes(lon, lat):
    def at(x, y):
        return (x % lon) * lat + y

    one, two = [], []
    for x in range(lon):
        for y in range(lat):
            one.append((at(x, y), at(x, y + 1 if y % 2 == 0 else y - 1)))
            if y == 0 or y == lat - 1:
                two.append((at(x, y), at(x + lon // 2, y)))
            else:
                two.append((at(x, y), at(x, y - 1 if y % 2 == 0 else y + 1)))
    return one, two


def place_numbers(height, first, last_row, rows):
    lat = lax.axis_index("lat")
    last = lax.axis_size("lat") - 1
    odd = lat % 2
    top = (lat == 0).astype(jnp.int32)
    bottom = (lat == last).astype(jnp.int32)
    h = height
    send_1 = [jnp.where(odd == 1, 0, h - 2), jnp.where(odd == 1, 1, h - 1)]
    send_2 = [
        jnp.where(odd == 1, h - 2 + bottom, top),
        jnp.where(odd == 1, h - 1 - bottom, 1 - top),
    ]
    got = [
        jnp.where(top == 1, 1, h - 2),
        jnp.where(top == 1, 0, h - 1),
        jnp.where(bottom == 1, h - 1, 0),
        jnp.where(bottom == 1, h - 2, 1),
    ]
    begin = (lax.axis_index("lon") * lax.axis_size("lat") + lat) * rows
    is_gain = jnp.logical_and(begin >= first, begin < last_row)
    values = send_1 + send_2 + got + [odd, top, bottom, is_gain]
    return jnp.stack([jnp.asarray(v, jnp.int32) for v in values])


def per_device(field, first_kernel, norm_gain, second_kernel, cotangent):
    channels, height, width = field.shape
    hid = norm_gain.shape[0]
    devices = lax.axis_size("lon") * lax.axis_size("lat")
    rows = -(-(4 * 5 * CP + hid) // (16 * devices)) * 16
    numbers = place_numbers(height, 4 * 5 * CP, 4 * 5 * CP + hid, rows)
    one, two = row_routes(lax.axis_size("lon"), lax.axis_size("lat"))
    us = 10**9

    main, low, high, rim_1, rim_2 = call(
        pack_kernel,
        [
            ((2, height, CP, 128), BF), ((2, CP, 128), BF), ((2, CP, 128), BF),
            ((2, 2, CP, 128), BF), ((2, 2, CP, 128), BF),
        ],
        [],
        (numbers, field, cotangent),
        5 * us,
        24,
    )
    right, left = exchange_columns(low, high)
    sides = jnp.stack([right, left], axis=1)
    rim_1, far_1 = lax.ppermute((rim_1, sides), AXES, one)
    rim_2, far_2 = lax.ppermute((rim_2, sides), AXES, two)

    w_1, w_2, w_3, w_4, spread = call(
        weights_kernel,
        [((5 * hid, 5 * CP), BF)] * 2 + [((5 * CP, 5 * hid), BF)] * 2 + [((hid, 128), F32)],
        [],
        (
            jnp.transpose(first_kernel, (2, 3, 0, 1)), jnp.transpose(second_kernel, (2, 3, 1, 0)),
            norm_gain[None],
        ),
        4 * us,
        16,
        numbers=False,
    )
    both, low, high, out_1, out_2, flat = call(
        first_kernel_body,
        [
            ((height, 2 * hid, 128), BF), ((2 * hid, 128), BF), ((2 * hid, 128), BF),
            ((2, 2 * hid, 128), BF), ((2, 2 * hid, 128), BF), ((rows * devices, 128), WIRE),
        ],
        [
            ((height, 5 * CP, 128), BF), ((height, 5 * CP, 128), BF),
            ((height + 8, hid, 128), F32), ((height + 8, hid, 128), F32),
            ((height + 8, hid, 128), BF), ((height + 8, hid, 128), BF),
            ((4, 5 * CP, 128), BF), ((4, 5 * CP, 128), BF),
            ((5 * CP, 256), BF), ((5 * CP, 256), BF),
            ((2, hid, 128), F32), ((2, hid, 128), F32),
        ],
        (
            numbers, main, right, left, rim_1, rim_2, far_1, far_2, w_1, w_2, spread,
        ),
        12 * us,
        48,
    )

    got = lax.all_to_all(flat.reshape(devices, rows, 128), AXES, 0, 0)
    right, left = exchange_columns(low, high)
    sides = jnp.stack([right, left], axis=0)
    out_1, far_1 = lax.ppermute((out_1, sides), AXES, one)
    out_2, far_2 = lax.ppermute((out_2, sides), AXES, two)
    factor = (height * width * devices) ** -0.5
    (mine,) = call(
        functools.partial(reduce_kernel, factor), [((devices, rows, 128), BF)], [],
        (numbers, got),
        10 * us,
        8,
    )
    mine, out_1, out_2, far_1, far_2 = lax.optimization_barrier((mine, out_1, out_2, far_1, far_2))
    summed = lax.all_to_all(mine, AXES, 0, 0).reshape(-1, 128)
    grad_1, grad_2, gain = call(
        unpack_kernel,
        [((5, 5, hid, channels), F32)] * 2 + [((1, hid), F32)],
        [],
        (summed,),
        20 * us,
        16,
        numbers=False,
    )
    grad_first = jnp.transpose(grad_1, (2, 3, 0, 1))
    grad_second = jnp.transpose(grad_2, (3, 2, 0, 1))

    results = []
    for which, weight, base in ((0, w_3, field), (1, w_4, cotangent)):
        results += call(
            functools.partial(second_kernel_body, which),
            [(field.shape, BF)],
            [((height + 4, 5 * hid, 128), BF), ((height + 8, CP, 128), F32)],
            (numbers, both, right, left, out_1, out_2, far_1, far_2, weight, base),
            2 * us,
            36,
        )
    return results[0], results[1], grad_first, grad_second, gain.reshape(hid)


def solution(mesh):
    placed = (P(None, "lat", "lon"), P(), P(), P(), P(None, "lat", "lon"))
    return jax.shard_map(
        per_device,
        mesh=mesh,
        in_specs=placed,
        out_specs=(P(None, "lat", "lon"), P(None, "lat", "lon"), P(), P(), P()),
        check_vma=False,
    )
```

```python
import functools

import jax
import jax.numpy as jnp
from jax import lax
from jax.experimental import pallas as pl
from jax.experimental.pallas import tpu as pltpu
from jax.sharding import PartitionSpec as P

EPS = 1e-05
BF = jnp.bfloat16
F32 = jnp.float32
AXES = ("lon", "lat")
CP = 80
WIRE = BF


def dot(a, b):
    return jnp.dot(a, b, preferred_element_type=F32)


def dot_nt(a, b):
    return lax.dot_general(a, b, (((1,), (1,)), ((), ())), preferred_element_type=F32)


def lanes_of(shape):
    return lax.broadcasted_iota(jnp.int32, shape, len(shape) - 1)


def edge_columns(read, rows, channels):
    pair = lanes_of((channels, 128)) // 2

    def body(r, found):
        low, high = found
        x = read(r)
        low = jnp.where(pair == r, pltpu.roll(x, 2 * r, 1), low)
        high = jnp.where(pair == r, pltpu.roll(x, lax.rem(2 * r + 2, 128), 1), high)
        return low, high

    zero = jnp.zeros((channels, 128), BF)
    return lax.fori_loop(0, rows, body, (zero, zero), unroll=rows)


def shifted(x, right, left, row):
    lane = lanes_of(x.shape)
    back = lax.rem(128 - 2 * row, 128)
    right = pltpu.roll(right, back, 1)
    left = pltpu.roll(left, lax.rem(254 - 2 * row, 128), 1)
    return [
        pltpu.roll(jnp.where(lane >= 126, left, x), 2, 1),
        pltpu.roll(jnp.where(lane >= 127, left, x), 1, 1),
        x,
        pltpu.roll(jnp.where(lane < 1, right, x), 127, 1),
        pltpu.roll(jnp.where(lane < 2, right, x), 126, 1),
    ]


def store_shifted(out, at, x, right, left, row):
    c = x.shape[0]
    for q, piece in enumerate(shifted(x, right, left, row)):
        out[at, q * c : (q + 1) * c, :] = piece


def fill_shifted(out, read_main, right, left, rows, halo):
    def body(r, carry):
        store_shifted(out, r + 2, read_main(r), right(), left(), r)
        return carry

    lax.fori_loop(0, rows, body, 0, unroll=rows)
    for at, x, far_right, far_left, row in halo:
        store_shifted(out, at, x, far_right, far_left, row)


def wide(ref, start, count):
    return jnp.concatenate([ref[start + t] for t in range(count)], axis=1)


def add_taps(acc, start, y, m, count, flip=None):
    for t in range(count):
        cols = slice(t * 128, (t + 1) * 128)
        for p in range(5):
            part = y[p * m : (p + 1) * m, cols]
            if flip is not None:
                part = jnp.where(flip[t], y[(4 - p) * m : (5 - p) * m, cols], part)
            acc[start[t] + 4 - p] = acc[start[t] + 4 - p] + part


def store_taps(acc, y, m, rows):
    for k in range(rows + 8):
        parts = [
            y[p * m : (p + 1) * m, (k - 6 + p) * 128 : (k - 5 + p) * 128]
            for p in range(5)
            if 0 <= k - 6 + p < rows
        ]
        acc[k] = sum(parts[1:], parts[0]) if parts else jnp.zeros(acc.shape[1:], F32)


def conv_rows(acc, stack, weight, m, rows, flip=None):
    y = dot(weight[...], wide(stack, 2, rows))
    store_taps(acc, y, m, rows)
    outer = (0, 1, rows + 2, rows + 3)
    y = dot(weight[...], jnp.concatenate([stack[i] for i in outer], axis=1))
    add_taps(acc, outer, y, m, 4, flip)


def row_stack(ref, i):
    return ref[pl.ds(i, 5)].reshape(5 * ref.shape[1], 128)


def correlate_outer(outer, grown, places, flip=None):
    pieces = []
    for t, i in enumerate(places):
        piece = row_stack(grown, i)
        if flip is not None:
            turned = jnp.concatenate([grown[i + 4 - m] for m in range(5)], axis=0)
            piece = jnp.where(flip[t], turned, piece)
        pieces.append(piece)
    return dot_nt(wide(outer, 0, 4), jnp.concatenate(pieces, axis=1))


def shifted_alone(x):
    lane = lanes_of(x.shape)
    zero = jnp.zeros_like(x)
    return [
        jnp.where(lane < 2, zero, pltpu.roll(x, 2, 1)),
        jnp.where(lane < 1, zero, pltpu.roll(x, 1, 1)),
        x,
        jnp.where(lane >= 127, zero, pltpu.roll(x, 127, 1)),
        jnp.where(lane >= 126, zero, pltpu.roll(x, 126, 1)),
    ]


def four_slots(high, low):
    source = lax.broadcasted_iota(jnp.int32, (256, 256), 0)
    target = lax.broadcasted_iota(jnp.int32, (256, 256), 1)
    side = (source >= 128).astype(jnp.int32)
    place = 4 * ((source - 128 * side) // 2) + source % 2 + 2 * side
    route = (target == place).astype(F32).astype(BF)
    return dot(jnp.concatenate([high, low], axis=1), route).astype(BF)


def edge_stack(right, left):
    c = right.shape[0]
    odd = lanes_of(right.shape) % 2 == 1
    zero = jnp.zeros_like(right)
    high = [zero, zero, zero, jnp.where(odd, pltpu.roll(right, 1, 1), zero), right]
    low = [left, jnp.where(odd, zero, pltpu.roll(left, 127, 1)), zero, zero, zero]
    return four_slots(jnp.concatenate(high, axis=0), jnp.concatenate(low, axis=0))


def slid(x, rows):
    by = 4 * rows
    if by == 0:
        return x
    lane = lanes_of(x.shape)
    inside = lane >= by if by > 0 else lane < 256 + by
    return jnp.where(inside, pltpu.roll(x, by % 256, 1), jnp.zeros_like(x))


def conv_alone(main, which, stack, weight, acc):
    height = main.shape[1]

    def body(r, carry):
        for q, piece in enumerate(shifted_alone(main[which, r])):
            stack[r, q * CP : (q + 1) * CP] = piece
        return carry

    lax.fori_loop(0, height, body, 0, unroll=8)
    y = dot(weight[...], wide(stack, 0, height))
    store_taps(acc, y, acc.shape[1], height)


def pack_kernel(rows_ref, field, cot, main, low, high, rim_1, rim_2):
    height = field.shape[1]
    lost = CP - field.shape[0]
    for which, source in enumerate((field, cot)):
        for b in range(height // 16):
            block = source[:, b * 16 : (b + 1) * 16, :].astype(F32)
            block = jnp.concatenate([block, jnp.zeros((lost, 16, 128), F32)], axis=0)
            main[which, b * 16 : (b + 1) * 16] = jnp.swapaxes(block, 0, 1).astype(BF)
        low[which], high[which] = edge_columns(lambda r: main[which, r], height, CP)
        for t in range(2):
            rim_1[which, t] = main[which, rows_ref[t]]
            rim_2[which, t] = main[which, rows_ref[2 + t]]


def halo_slabs(rows_ref, odd, rim_1, rim_2, far_1, far_2, which):
    got = []
    for side in range(2):
        upper = side == 0
        pick = odd if upper else jnp.logical_not(odd)
        far = [jnp.where(pick, far_1[which, k], far_2[which, k]) for k in range(2)]
        for t in range(2):
            slab = jnp.where(pick, rim_1[which, t], rim_2[which, t])
            got.append((slab, far[0], far[1], rows_ref[4 + 2 * side + t]))
    return got


def first_kernel_body(
    rows_ref, main, right, left, rim_1, rim_2, far_1, far_2, w_1, w_2, gain,
    both, low, high, out_1, out_2, flat,
    stack_1, stack_2, acc_1, acc_2, grown_1, grown_2, outer_1, outer_2, edge_1, edge_2, z_1, z_2,
):
    height, _, _ = both.shape
    hid = gain.shape[0]
    odd = rows_ref[8] == 1
    top = rows_ref[9] == 1
    bottom = rows_ref[10] == 1
    flip = (top, top, bottom, bottom)
    places = (0, 1, height + 2, height + 3)
    for grown in (grown_1, grown_2):
        grown[0:4] = jnp.zeros((4, hid, 128), BF)
        grown[height + 4 : height + 8] = jnp.zeros((4, hid, 128), BF)
    weights = (w_1, w_2)
    for which, (outer, edge, z) in enumerate(((outer_1, edge_1, z_1), (outer_2, edge_2, z_2))):
        halo = halo_slabs(rows_ref, odd, rim_1, rim_2, far_1, far_2, which)
        for t in range(4):
            store_shifted(outer, t, *halo[t])
        edge[...] = edge_stack(right[which], left[which])
        y = dot(weights[which][...], edge[...])
        found = sum(slid(y[p * hid : (p + 1) * hid], 2 - p) for p in range(5))
        z[0] = found[:, 0:128]
        z[1] = found[:, 128:256]
    conv_alone(main, 0, stack_1, w_1, acc_1)
    conv_alone(main, 1, stack_2, w_2, acc_2)
    for which, (outer, acc) in enumerate(((outer_1, acc_1), (outer_2, acc_2))):
        y = dot(weights[which][...], wide(outer, 0, 4))
        add_taps(acc, places, y, hid, 4, flip if which == 1 else None)
    spread = gain[...]
    lane = lanes_of((hid, 128))
    side = jnp.logical_or(lane < 2, lane >= 126)

    def cells(r, total):
        turn = lax.rem(382 - 4 * r, 128)

        def with_edges(acc, z):
            return acc[r + 4] + jnp.where(side, pltpu.roll(z[r // 32], turn, 1), 0.0)

        pre = with_edges(acc_1, z_1)
        grad_act = with_edges(acc_2, z_2)
        scale = lax.rsqrt(jnp.mean(pre * pre, axis=0, keepdims=True) + EPS)
        unit = pre * scale
        normed = unit * spread
        sig = 1.0 / (1.0 + jnp.exp(-normed))
        active = (normed * sig).astype(BF)
        grad_normed = grad_act * sig * (1.0 + normed * (1.0 - sig))
        g2 = grad_normed * spread
        mean = jnp.mean(g2 * pre, axis=0, keepdims=True)
        grad_pre = (scale * g2 - pre * (scale * scale * scale * mean)).astype(BF)
        grown_1[r + 4] = grad_pre
        grown_2[r + 4] = active
        both[r, 0:hid] = active
        both[r, hid : 2 * hid] = grad_pre
        return total + grad_normed * unit

    total = lax.fori_loop(0, height, cells, jnp.zeros((hid, 128), F32), unroll=16)
    lows, highs = edge_columns(lambda r: both[r], height, 2 * hid)
    low[...] = lows
    high[...] = highs
    for t in range(2):
        out_1[t] = both[rows_ref[t]]
        out_2[t] = both[rows_ref[2 + t]]
    m = 5 * CP
    slots = four_slots(highs, lows)
    spare = jnp.zeros((m, 256 - 5 * hid), F32)
    for which, (stack, outer, edge, grown) in enumerate(
        ((stack_1, outer_1, edge_1, grown_1), (stack_2, outer_2, edge_2, grown_2))
    ):
        mine = slots[hid:] if which == 0 else slots[:hid]
        mine = jnp.concatenate([slid(mine.astype(F32), 2 - k).astype(BF) for k in range(5)], axis=0)
        found = dot_nt(edge[...], mine)
        found = found + correlate_outer(outer, grown, places, flip if which == 1 else None)
        right_side = jnp.concatenate([row_stack(grown, i + 2) for i in range(height)], axis=1)
        found = found + dot_nt(wide(stack, 0, height), right_side)
        found = jnp.concatenate([found, spare], axis=1).astype(WIRE)
        flat[2 * which * m : (2 * which + 1) * m] = found[:, 0:128]
        flat[(2 * which + 1) * m : (2 * which + 2) * m] = found[:, 128:256]
    used = flat.shape[0] - 4 * m
    total = jnp.broadcast_to(jnp.sum(total, axis=1, keepdims=True), (hid, 128))
    coarse = total.astype(WIRE)
    total = jnp.where(lane < 64, coarse, (total - coarse.astype(F32)).astype(WIRE))
    flat[4 * m :] = jnp.concatenate([total, jnp.zeros((used - hid, 128), WIRE)], axis=0)


def second_kernel_body(
    which, rows_ref, both, right, left, rim_1, rim_2, far_1, far_2, weight, base, out, stack, acc,
):
    height = base.shape[1]
    channels = base.shape[0]
    hid = both.shape[1] // 2
    odd = rows_ref[8] == 1
    top = rows_ref[9] == 1
    bottom = rows_ref[10] == 1
    outer = (0, 1, height + 2, height + 3)
    part = slice(which * hid, (which + 1) * hid)
    halo = []
    for side in range(2):
        pick = odd if side == 0 else jnp.logical_not(odd)
        far = [jnp.where(pick, far_1[k, part], far_2[k, part]) for k in range(2)]
        for t in range(2):
            slab = jnp.where(pick, rim_1[t, part], rim_2[t, part])
            halo.append((outer[2 * side + t], slab, far[0], far[1], rows_ref[4 + 2 * side + t]))
    fill_shifted(
        stack, lambda r: both[r, part], lambda: right[part], lambda: left[part], height, halo
    )
    flip = (top, top, bottom, bottom) if which == 1 else None
    conv_rows(acc, stack, weight, CP, height, flip)
    for b in range(height // 16):
        rows = slice(b * 16, (b + 1) * 16)
        block = jnp.swapaxes(acc[b * 16 + 4 : b * 16 + 20], 0, 1)[0:channels]
        out[:, rows, :] = (base[:, rows, :].astype(F32) + block).astype(BF)


def weights_kernel(k_1, k_2, gain, w_1, w_2, w_3, w_4, spread):
    hid, channels = k_1.shape[2:]
    gap = jnp.zeros((hid, CP - channels), F32)
    spread[...] = jnp.broadcast_to(gain[...], (128, hid)).T

    def plane(k, p, q):
        return jnp.concatenate([k[p, q].astype(F32), gap], axis=1)

    for p in range(5):
        rows = slice(p * hid, (p + 1) * hid)
        w_1[rows] = jnp.concatenate([plane(k_1, p, q) for q in range(5)], axis=1).astype(BF)
        w_2[rows] = jnp.concatenate([plane(k_2, 4 - p, 4 - q) for q in range(5)], axis=1).astype(BF)
        rows = slice(p * CP, (p + 1) * CP)
        w_3[rows] = jnp.concatenate([plane(k_2, p, q) for q in range(5)], axis=0).T.astype(BF)
        w_4[rows] = jnp.concatenate([plane(k_1, 4 - p, 4 - q) for q in range(5)], axis=0).T.astype(BF)


def reduce_kernel(factor, rows_ref, got, out):
    devices = got.shape[0]

    def body(i, total):
        return total + got[i].astype(F32)

    total = lax.fori_loop(0, devices, body, jnp.zeros(got.shape[1:], F32), unroll=16)
    mine = (total * factor).astype(BF)
    whole = (total + pltpu.roll(total, 64, 1)) * factor
    coarse = whole.astype(BF)
    fine = (whole - coarse.astype(F32)).astype(BF)
    pair = jnp.where(lanes_of(total.shape) < 64, coarse, fine)
    mine = jnp.where(rows_ref[11] == 1, pair, mine)
    for i in range(devices):
        out[i] = mine


def unpack_kernel(rows, grad_1, grad_2, gain):
    hid, channels = grad_1.shape[2:]
    m = 5 * CP
    for which in range(2):
        at = 2 * which * m
        low = rows[at : at + m].astype(F32).T
        high = rows[at + m : at + 2 * m].astype(F32).T
        both = jnp.concatenate([low, high], axis=0)
        for q in range(5):
            part = both[0 : 5 * hid, q * CP : q * CP + channels]
            for t in range(5):
                piece = part[t * hid : (t + 1) * hid]
                if which == 0:
                    grad_1[4 - t, q] = piece
                else:
                    grad_2[t, 4 - q] = piece
    pair = rows[4 * m : 4 * m + hid].astype(F32).T
    gain[...] = pair[0:1] + pair[64:65]


def call(body, outs, scratch, args, flops, mib, numbers=True):
    near = pl.BlockSpec(memory_space=pltpu.VMEM)
    in_specs = [near] * len(args)
    if numbers:
        in_specs[0] = pl.BlockSpec(memory_space=pltpu.SMEM)
    return pl.pallas_call(
        body,
        out_shape=[jax.ShapeDtypeStruct(s, t) for s, t in outs],
        in_specs=in_specs,
        out_specs=[near] * len(outs),
        scratch_shapes=[pltpu.VMEM(s, t) for s, t in scratch],
        compiler_params=pltpu.CompilerParams(vmem_limit_bytes=mib << 20),
        cost_estimate=pl.CostEstimate(flops=flops, bytes_accessed=1 << 20, transcendentals=0),
    )(*args)


def exchange_columns(low, high):
    count = lax.axis_size("lon")
    up = [(i, (i + 1) % count) for i in range(count)]
    down = [(t, s) for s, t in up]
    right = lax.ppermute(low, "lon", down)
    left = lax.ppermute(high, "lon", up)
    return right, left


def row_routes(lon, lat):
    def at(x, y):
        return (x % lon) * lat + y

    one, two = [], []
    for x in range(lon):
        for y in range(lat):
            one.append((at(x, y), at(x, y + 1 if y % 2 == 0 else y - 1)))
            if y == 0 or y == lat - 1:
                two.append((at(x, y), at(x + lon // 2, y)))
            else:
                two.append((at(x, y), at(x, y - 1 if y % 2 == 0 else y + 1)))
    return one, two


def place_numbers(height, first, last_row, rows):
    lat = lax.axis_index("lat")
    last = lax.axis_size("lat") - 1
    odd = lat % 2
    top = (lat == 0).astype(jnp.int32)
    bottom = (lat == last).astype(jnp.int32)
    h = height
    send_1 = [jnp.where(odd == 1, 0, h - 2), jnp.where(odd == 1, 1, h - 1)]
    send_2 = [
        jnp.where(odd == 1, h - 2 + bottom, top),
        jnp.where(odd == 1, h - 1 - bottom, 1 - top),
    ]
    got = [
        jnp.where(top == 1, 1, h - 2),
        jnp.where(top == 1, 0, h - 1),
        jnp.where(bottom == 1, h - 1, 0),
        jnp.where(bottom == 1, h - 2, 1),
    ]
    begin = (lax.axis_index("lon") * lax.axis_size("lat") + lat) * rows
    is_gain = jnp.logical_and(begin >= first, begin < last_row)
    values = send_1 + send_2 + got + [odd, top, bottom, is_gain]
    return jnp.stack([jnp.asarray(v, jnp.int32) for v in values])


def per_device(field, first_kernel, norm_gain, second_kernel, cotangent):
    channels, height, width = field.shape
    hid = norm_gain.shape[0]
    devices = lax.axis_size("lon") * lax.axis_size("lat")
    rows = -(-(4 * 5 * CP + hid) // (16 * devices)) * 16
    numbers = place_numbers(height, 4 * 5 * CP, 4 * 5 * CP + hid, rows)
    one, two = row_routes(lax.axis_size("lon"), lax.axis_size("lat"))
    us = 10**9

    main, low, high, rim_1, rim_2 = call(
        pack_kernel,
        [
            ((2, height, CP, 128), BF), ((2, CP, 128), BF), ((2, CP, 128), BF),
            ((2, 2, CP, 128), BF), ((2, 2, CP, 128), BF),
        ],
        [],
        (numbers, field, cotangent),
        5 * us,
        24,
    )
    right, left = exchange_columns(low, high)
    sides = jnp.stack([right, left], axis=1)
    rim_1, far_1 = lax.ppermute((rim_1, sides), AXES, one)
    rim_2, far_2 = lax.ppermute((rim_2, sides), AXES, two)

    w_1, w_2, w_3, w_4, spread = call(
        weights_kernel,
        [((5 * hid, 5 * CP), BF)] * 2 + [((5 * CP, 5 * hid), BF)] * 2 + [((hid, 128), F32)],
        [],
        (
            jnp.transpose(first_kernel, (2, 3, 0, 1)), jnp.transpose(second_kernel, (2, 3, 1, 0)),
            norm_gain[None],
        ),
        4 * us,
        16,
        numbers=False,
    )
    both, low, high, out_1, out_2, flat = call(
        first_kernel_body,
        [
            ((height, 2 * hid, 128), BF), ((2 * hid, 128), BF), ((2 * hid, 128), BF),
            ((2, 2 * hid, 128), BF), ((2, 2 * hid, 128), BF), ((rows * devices, 128), WIRE),
        ],
        [
            ((height, 5 * CP, 128), BF), ((height, 5 * CP, 128), BF),
            ((height + 8, hid, 128), F32), ((height + 8, hid, 128), F32),
            ((height + 8, hid, 128), BF), ((height + 8, hid, 128), BF),
            ((4, 5 * CP, 128), BF), ((4, 5 * CP, 128), BF),
            ((5 * CP, 256), BF), ((5 * CP, 256), BF),
            ((2, hid, 128), F32), ((2, hid, 128), F32),
        ],
        (
            numbers, main, right, left, rim_1, rim_2, far_1, far_2, w_1, w_2, spread,
        ),
        12 * us,
        34,
    )

    got = lax.all_to_all(flat.reshape(devices, rows, 128), AXES, 0, 0)
    right, left = exchange_columns(low, high)
    sides = jnp.stack([right, left], axis=0)
    out_1, far_1 = lax.ppermute((out_1, sides), AXES, one)
    out_2, far_2 = lax.ppermute((out_2, sides), AXES, two)
    factor = (height * width * devices) ** -0.5
    (mine,) = call(
        functools.partial(reduce_kernel, factor), [((devices, rows, 128), BF)], [],
        (numbers, got),
        10 * us,
        8,
    )
    mine, out_1, out_2, far_1, far_2 = lax.optimization_barrier((mine, out_1, out_2, far_1, far_2))
    summed = lax.all_to_all(mine, AXES, 0, 0).reshape(-1, 128)
    grad_1, grad_2, gain = call(
        unpack_kernel,
        [((5, 5, hid, channels), F32)] * 2 + [((1, hid), F32)],
        [],
        (summed,),
        20 * us,
        16,
        numbers=False,
    )
    grad_first = jnp.transpose(grad_1, (2, 3, 0, 1))
    grad_second = jnp.transpose(grad_2, (3, 2, 0, 1))

    results = []
    for which, weight, base in ((0, w_3, field), (1, w_4, cotangent)):
        results += call(
            functools.partial(second_kernel_body, which),
            [(field.shape, BF)],
            [((height + 4, 5 * hid, 128), BF), ((height + 8, CP, 128), F32)],
            (numbers, both, right, left, out_1, out_2, far_1, far_2, weight, base),
            2 * us,
            28,
        )
    return results[0], results[1], grad_first, grad_second, gain.reshape(hid)


def solution(mesh):
    placed = (P(None, "lat", "lon"), P(), P(), P(), P(None, "lat", "lon"))
    return jax.shard_map(
        per_device,
        mesh=mesh,
        in_specs=placed,
        out_specs=(P(None, "lat", "lon"), P(None, "lat", "lon"), P(), P(), P()),
        check_vma=False,
    )
```

```python
import functools

import jax
import jax.numpy as jnp
from jax import lax
from jax.experimental import pallas as pl
from jax.experimental.pallas import tpu as pltpu
from jax.sharding import PartitionSpec as P

EPS = 1e-05
BF = jnp.bfloat16
F32 = jnp.float32
AXES = ("lon", "lat")
CP = 80
WIRE = BF


def dot(a, b):
    return jnp.dot(a, b, preferred_element_type=F32)


def dot_nt(a, b):
    return lax.dot_general(a, b, (((1,), (1,)), ((), ())), preferred_element_type=F32)


def lanes_of(shape):
    return lax.broadcasted_iota(jnp.int32, shape, len(shape) - 1)


def edge_columns(read, rows, channels):
    pair = lanes_of((channels, 128)) // 2

    def body(r, found):
        low, high = found
        x = read(r)
        low = jnp.where(pair == r, pltpu.roll(x, 2 * r, 1), low)
        high = jnp.where(pair == r, pltpu.roll(x, lax.rem(2 * r + 2, 128), 1), high)
        return low, high

    zero = jnp.zeros((channels, 128), BF)
    return lax.fori_loop(0, rows, body, (zero, zero), unroll=rows)


def shifted(x, right, left, row):
    lane = lanes_of(x.shape)
    back = lax.rem(128 - 2 * row, 128)
    right = pltpu.roll(right, back, 1)
    left = pltpu.roll(left, lax.rem(254 - 2 * row, 128), 1)
    return [
        pltpu.roll(jnp.where(lane >= 126, left, x), 2, 1),
        pltpu.roll(jnp.where(lane >= 127, left, x), 1, 1),
        x,
        pltpu.roll(jnp.where(lane < 1, right, x), 127, 1),
        pltpu.roll(jnp.where(lane < 2, right, x), 126, 1),
    ]


def store_shifted(out, at, x, right, left, row):
    c = x.shape[0]
    for q, piece in enumerate(shifted(x, right, left, row)):
        out[at, q * c : (q + 1) * c, :] = piece


def fill_shifted(out, read_main, right, left, rows, halo):
    def body(r, carry):
        store_shifted(out, r + 2, read_main(r), right(), left(), r)
        return carry

    lax.fori_loop(0, rows, body, 0, unroll=rows)
    for at, x, far_right, far_left, row in halo:
        store_shifted(out, at, x, far_right, far_left, row)


def wide(ref, start, count):
    return jnp.concatenate([ref[start + t] for t in range(count)], axis=1)


def add_taps(acc, start, y, m, count, flip=None):
    for t in range(count):
        cols = slice(t * 128, (t + 1) * 128)
        for p in range(5):
            part = y[p * m : (p + 1) * m, cols]
            if flip is not None:
                part = jnp.where(flip[t], y[(4 - p) * m : (5 - p) * m, cols], part)
            acc[start[t] + 4 - p] = acc[start[t] + 4 - p] + part


def store_taps(acc, y, m, rows):
    for k in range(rows + 8):
        parts = [
            y[p * m : (p + 1) * m, (k - 6 + p) * 128 : (k - 5 + p) * 128]
            for p in range(5)
            if 0 <= k - 6 + p < rows
        ]
        acc[k] = sum(parts[1:], parts[0]) if parts else jnp.zeros(acc.shape[1:], F32)


def conv_rows(acc, stack, weight, m, rows, flip=None):
    y = dot(weight[...], wide(stack, 2, rows))
    store_taps(acc, y, m, rows)
    outer = (0, 1, rows + 2, rows + 3)
    y = dot(weight[...], jnp.concatenate([stack[i] for i in outer], axis=1))
    add_taps(acc, outer, y, m, 4, flip)


def row_stack(ref, i):
    return ref[pl.ds(i, 5)].reshape(5 * ref.shape[1], 128)


def correlate_outer(outer, grown, places, flip=None):
    pieces = []
    for t, i in enumerate(places):
        piece = row_stack(grown, i)
        if flip is not None:
            turned = jnp.concatenate([grown[i + 4 - m] for m in range(5)], axis=0)
            piece = jnp.where(flip[t], turned, piece)
        pieces.append(piece)
    return dot_nt(wide(outer, 0, 4), jnp.concatenate(pieces, axis=1))


def shifted_alone(x):
    lane = lanes_of(x.shape)
    zero = jnp.zeros_like(x)
    return [
        jnp.where(lane < 2, zero, pltpu.roll(x, 2, 1)),
        jnp.where(lane < 1, zero, pltpu.roll(x, 1, 1)),
        x,
        jnp.where(lane >= 127, zero, pltpu.roll(x, 127, 1)),
        jnp.where(lane >= 126, zero, pltpu.roll(x, 126, 1)),
    ]


def four_slots(high, low):
    source = lax.broadcasted_iota(jnp.int32, (256, 256), 0)
    target = lax.broadcasted_iota(jnp.int32, (256, 256), 1)
    side = (source >= 128).astype(jnp.int32)
    place = 4 * ((source - 128 * side) // 2) + source % 2 + 2 * side
    route = (target == place).astype(F32).astype(BF)
    return dot(jnp.concatenate([high, low], axis=1), route).astype(BF)


def edge_stack(right, left):
    c = right.shape[0]
    odd = lanes_of(right.shape) % 2 == 1
    zero = jnp.zeros_like(right)
    high = [zero, zero, zero, jnp.where(odd, pltpu.roll(right, 1, 1), zero), right]
    low = [left, jnp.where(odd, zero, pltpu.roll(left, 127, 1)), zero, zero, zero]
    return four_slots(jnp.concatenate(high, axis=0), jnp.concatenate(low, axis=0))


def slid(x, rows):
    by = 4 * rows
    if by == 0:
        return x
    lane = lanes_of(x.shape)
    inside = lane >= by if by > 0 else lane < 256 + by
    return jnp.where(inside, pltpu.roll(x, by % 256, 1), jnp.zeros_like(x))


def conv_alone(main, which, stack, weight, acc):
    height = main.shape[1]

    def body(r, carry):
        for q, piece in enumerate(shifted_alone(main[which, r])):
            stack[r, q * CP : (q + 1) * CP] = piece
        return carry

    lax.fori_loop(0, height, body, 0, unroll=32)
    y = dot(weight[...], wide(stack, 0, height))
    store_taps(acc, y, acc.shape[1], height)


def pack_kernel(rows_ref, field, cot, main, low, high, rim_1, rim_2):
    height = field.shape[1]
    lost = CP - field.shape[0]
    for which, source in enumerate((field, cot)):
        for b in range(height // 16):
            block = source[:, b * 16 : (b + 1) * 16, :].astype(F32)
            block = jnp.concatenate([block, jnp.zeros((lost, 16, 128), F32)], axis=0)
            main[which, b * 16 : (b + 1) * 16] = jnp.swapaxes(block, 0, 1).astype(BF)
        low[which], high[which] = edge_columns(lambda r: main[which, r], height, CP)
        for t in range(2):
            rim_1[which, t] = main[which, rows_ref[t]]
            rim_2[which, t] = main[which, rows_ref[2 + t]]


def halo_slabs(rows_ref, odd, rim_1, rim_2, far_1, far_2, which):
    got = []
    for side in range(2):
        upper = side == 0
        pick = odd if upper else jnp.logical_not(odd)
        far = [jnp.where(pick, far_1[which, k], far_2[which, k]) for k in range(2)]
        for t in range(2):
            slab = jnp.where(pick, rim_1[which, t], rim_2[which, t])
            got.append((slab, far[0], far[1], rows_ref[4 + 2 * side + t]))
    return got


def first_kernel_body(
    rows_ref, main, right, left, rim_1, rim_2, far_1, far_2, w_1, w_2, gain,
    both, low, high, out_1, out_2, flat,
    stack_1, stack_2, acc_1, acc_2, grown_1, grown_2, outer_1, outer_2, edge_1, edge_2, z_1, z_2,
):
    height, _, _ = both.shape
    hid = gain.shape[0]
    odd = rows_ref[8] == 1
    top = rows_ref[9] == 1
    bottom = rows_ref[10] == 1
    flip = (top, top, bottom, bottom)
    places = (0, 1, height + 2, height + 3)
    for grown in (grown_1, grown_2):
        grown[0:4] = jnp.zeros((4, hid, 128), BF)
        grown[height + 4 : height + 8] = jnp.zeros((4, hid, 128), BF)
    weights = (w_1, w_2)
    for which, (outer, edge, z) in enumerate(((outer_1, edge_1, z_1), (outer_2, edge_2, z_2))):
        halo = halo_slabs(rows_ref, odd, rim_1, rim_2, far_1, far_2, which)
        for t in range(4):
            store_shifted(outer, t, *halo[t])
        edge[...] = edge_stack(right[which], left[which])
        y = dot(weights[which][...], edge[...])
        found = sum(slid(y[p * hid : (p + 1) * hid], 2 - p) for p in range(5))
        z[0] = found[:, 0:128]
        z[1] = found[:, 128:256]
    conv_alone(main, 0, stack_1, w_1, acc_1)
    conv_alone(main, 1, stack_2, w_2, acc_2)
    for which, (outer, acc) in enumerate(((outer_1, acc_1), (outer_2, acc_2))):
        y = dot(weights[which][...], wide(outer, 0, 4))
        add_taps(acc, places, y, hid, 4, flip if which == 1 else None)
    spread = gain[...]
    lane = lanes_of((hid, 128))
    side = jnp.logical_or(lane < 2, lane >= 126)

    def cells(r, total):
        turn = lax.rem(382 - 4 * r, 128)

        def with_edges(acc, z):
            return acc[r + 4] + jnp.where(side, pltpu.roll(z[r // 32], turn, 1), 0.0)

        pre = with_edges(acc_1, z_1)
        grad_act = with_edges(acc_2, z_2)
        scale = lax.rsqrt(jnp.mean(pre * pre, axis=0, keepdims=True) + EPS)
        unit = pre * scale
        normed = unit * spread
        sig = 1.0 / (1.0 + jnp.exp(-normed))
        active = (normed * sig).astype(BF)
        grad_normed = grad_act * sig * (1.0 + normed * (1.0 - sig))
        g2 = grad_normed * spread
        mean = jnp.mean(g2 * pre, axis=0, keepdims=True)
        grad_pre = (scale * g2 - pre * (scale * scale * scale * mean)).astype(BF)
        grown_1[r + 4] = grad_pre
        grown_2[r + 4] = active
        both[r, 0:hid] = active
        both[r, hid : 2 * hid] = grad_pre
        return total + grad_normed * unit

    total = lax.fori_loop(0, height, cells, jnp.zeros((hid, 128), F32), unroll=32)
    lows, highs = edge_columns(lambda r: both[r], height, 2 * hid)
    low[...] = lows
    high[...] = highs
    for t in range(2):
        out_1[t] = both[rows_ref[t]]
        out_2[t] = both[rows_ref[2 + t]]
    m = 5 * CP
    slots = four_slots(highs, lows)
    spare = jnp.zeros((m, 256 - 5 * hid), F32)
    for which, (stack, outer, edge, grown) in enumerate(
        ((stack_1, outer_1, edge_1, grown_1), (stack_2, outer_2, edge_2, grown_2))
    ):
        mine = slots[hid:] if which == 0 else slots[:hid]
        mine = jnp.concatenate([slid(mine.astype(F32), 2 - k).astype(BF) for k in range(5)], axis=0)
        found = dot_nt(edge[...], mine)
        found = found + correlate_outer(outer, grown, places, flip if which == 1 else None)
        right_side = jnp.concatenate([row_stack(grown, i + 2) for i in range(height)], axis=1)
        found = found + dot_nt(wide(stack, 0, height), right_side)
        found = jnp.concatenate([found, spare], axis=1).astype(WIRE)
        flat[2 * which * m : (2 * which + 1) * m] = found[:, 0:128]
        flat[(2 * which + 1) * m : (2 * which + 2) * m] = found[:, 128:256]
    used = flat.shape[0] - 4 * m
    total = jnp.broadcast_to(jnp.sum(total, axis=1, keepdims=True), (hid, 128))
    coarse = total.astype(WIRE)
    total = jnp.where(lane < 64, coarse, (total - coarse.astype(F32)).astype(WIRE))
    flat[4 * m :] = jnp.concatenate([total, jnp.zeros((used - hid, 128), WIRE)], axis=0)


def second_kernel_body(
    which, rows_ref, both, right, left, rim_1, rim_2, far_1, far_2, weight, base, out, stack, acc,
):
    height = base.shape[1]
    channels = base.shape[0]
    hid = both.shape[1] // 2
    odd = rows_ref[8] == 1
    top = rows_ref[9] == 1
    bottom = rows_ref[10] == 1
    outer = (0, 1, height + 2, height + 3)
    part = slice(which * hid, (which + 1) * hid)
    halo = []
    for side in range(2):
        pick = odd if side == 0 else jnp.logical_not(odd)
        far = [jnp.where(pick, far_1[k, part], far_2[k, part]) for k in range(2)]
        for t in range(2):
            slab = jnp.where(pick, rim_1[t, part], rim_2[t, part])
            halo.append((outer[2 * side + t], slab, far[0], far[1], rows_ref[4 + 2 * side + t]))
    fill_shifted(
        stack, lambda r: both[r, part], lambda: right[part], lambda: left[part], height, halo
    )
    flip = (top, top, bottom, bottom) if which == 1 else None
    conv_rows(acc, stack, weight, CP, height, flip)
    for b in range(height // 16):
        rows = slice(b * 16, (b + 1) * 16)
        block = jnp.swapaxes(acc[b * 16 + 4 : b * 16 + 20], 0, 1)[0:channels]
        out[:, rows, :] = (base[:, rows, :].astype(F32) + block).astype(BF)


def weights_kernel(k_1, k_2, gain, w_1, w_2, w_3, w_4, spread):
    hid, channels = k_1.shape[2:]
    gap = jnp.zeros((hid, CP - channels), F32)
    spread[...] = jnp.broadcast_to(gain[...], (128, hid)).T

    def plane(k, p, q):
        return jnp.concatenate([k[p, q].astype(F32), gap], axis=1)

    for p in range(5):
        rows = slice(p * hid, (p + 1) * hid)
        w_1[rows] = jnp.concatenate([plane(k_1, p, q) for q in range(5)], axis=1).astype(BF)
        w_2[rows] = jnp.concatenate([plane(k_2, 4 - p, 4 - q) for q in range(5)], axis=1).astype(BF)
        rows = slice(p * CP, (p + 1) * CP)
        w_3[rows] = jnp.concatenate([plane(k_2, p, q) for q in range(5)], axis=0).T.astype(BF)
        w_4[rows] = jnp.concatenate([plane(k_1, 4 - p, 4 - q) for q in range(5)], axis=0).T.astype(BF)


def reduce_kernel(factor, rows_ref, got, out):
    devices = got.shape[0]

    def body(i, total):
        return total + got[i].astype(F32)

    total = lax.fori_loop(0, devices, body, jnp.zeros(got.shape[1:], F32), unroll=16)
    mine = (total * factor).astype(BF)
    whole = (total + pltpu.roll(total, 64, 1)) * factor
    coarse = whole.astype(BF)
    fine = (whole - coarse.astype(F32)).astype(BF)
    pair = jnp.where(lanes_of(total.shape) < 64, coarse, fine)
    mine = jnp.where(rows_ref[11] == 1, pair, mine)
    for i in range(devices):
        out[i] = mine


def unpack_kernel(rows, grad_1, grad_2, gain):
    hid, channels = grad_1.shape[2:]
    m = 5 * CP
    for which in range(2):
        at = 2 * which * m
        low = rows[at : at + m].astype(F32).T
        high = rows[at + m : at + 2 * m].astype(F32).T
        both = jnp.concatenate([low, high], axis=0)
        for q in range(5):
            part = both[0 : 5 * hid, q * CP : q * CP + channels]
            for t in range(5):
                piece = part[t * hid : (t + 1) * hid]
                if which == 0:
                    grad_1[4 - t, q] = piece
                else:
                    grad_2[t, 4 - q] = piece
    pair = rows[4 * m : 4 * m + hid].astype(F32).T
    gain[...] = pair[0:1] + pair[64:65]


def call(body, outs, scratch, args, flops, mib, numbers=True):
    near = pl.BlockSpec(memory_space=pltpu.VMEM)
    in_specs = [near] * len(args)
    if numbers:
        in_specs[0] = pl.BlockSpec(memory_space=pltpu.SMEM)
    return pl.pallas_call(
        body,
        out_shape=[jax.ShapeDtypeStruct(s, t) for s, t in outs],
        in_specs=in_specs,
        out_specs=[near] * len(outs),
        scratch_shapes=[pltpu.VMEM(s, t) for s, t in scratch],
        compiler_params=pltpu.CompilerParams(vmem_limit_bytes=mib << 20),
        cost_estimate=pl.CostEstimate(flops=flops, bytes_accessed=1 << 20, transcendentals=0),
    )(*args)


def exchange_columns(low, high):
    count = lax.axis_size("lon")
    up = [(i, (i + 1) % count) for i in range(count)]
    down = [(t, s) for s, t in up]
    right = lax.ppermute(low, "lon", down)
    left = lax.ppermute(high, "lon", up)
    return right, left


def row_routes(lon, lat):
    def at(x, y):
        return (x % lon) * lat + y

    one, two = [], []
    for x in range(lon):
        for y in range(lat):
            one.append((at(x, y), at(x, y + 1 if y % 2 == 0 else y - 1)))
            if y == 0 or y == lat - 1:
                two.append((at(x, y), at(x + lon // 2, y)))
            else:
                two.append((at(x, y), at(x, y - 1 if y % 2 == 0 else y + 1)))
    return one, two


def place_numbers(height, first, last_row, rows):
    lat = lax.axis_index("lat")
    last = lax.axis_size("lat") - 1
    odd = lat % 2
    top = (lat == 0).astype(jnp.int32)
    bottom = (lat == last).astype(jnp.int32)
    h = height
    send_1 = [jnp.where(odd == 1, 0, h - 2), jnp.where(odd == 1, 1, h - 1)]
    send_2 = [
        jnp.where(odd == 1, h - 2 + bottom, top),
        jnp.where(odd == 1, h - 1 - bottom, 1 - top),
    ]
    got = [
        jnp.where(top == 1, 1, h - 2),
        jnp.where(top == 1, 0, h - 1),
        jnp.where(bottom == 1, h - 1, 0),
        jnp.where(bottom == 1, h - 2, 1),
    ]
    begin = (lax.axis_index("lon") * lax.axis_size("lat") + lat) * rows
    is_gain = jnp.logical_and(begin >= first, begin < last_row)
    values = send_1 + send_2 + got + [odd, top, bottom, is_gain]
    return jnp.stack([jnp.asarray(v, jnp.int32) for v in values])


def per_device(field, first_kernel, norm_gain, second_kernel, cotangent):
    channels, height, width = field.shape
    hid = norm_gain.shape[0]
    devices = lax.axis_size("lon") * lax.axis_size("lat")
    rows = -(-(4 * 5 * CP + hid) // (16 * devices)) * 16
    numbers = place_numbers(height, 4 * 5 * CP, 4 * 5 * CP + hid, rows)
    one, two = row_routes(lax.axis_size("lon"), lax.axis_size("lat"))
    us = 10**9

    main, low, high, rim_1, rim_2 = call(
        pack_kernel,
        [
            ((2, height, CP, 128), BF), ((2, CP, 128), BF), ((2, CP, 128), BF),
            ((2, 2, CP, 128), BF), ((2, 2, CP, 128), BF),
        ],
        [],
        (numbers, field, cotangent),
        5 * us,
        24,
    )
    right, left = exchange_columns(low, high)
    sides = jnp.stack([right, left], axis=1)
    rim_1, far_1 = lax.ppermute((rim_1, sides), AXES, one)
    rim_2, far_2 = lax.ppermute((rim_2, sides), AXES, two)

    w_1, w_2, w_3, w_4, spread = call(
        weights_kernel,
        [((5 * hid, 5 * CP), BF)] * 2 + [((5 * CP, 5 * hid), BF)] * 2 + [((hid, 128), F32)],
        [],
        (
            jnp.transpose(first_kernel, (2, 3, 0, 1)), jnp.transpose(second_kernel, (2, 3, 1, 0)),
            norm_gain[None],
        ),
        4 * us,
        16,
        numbers=False,
    )
    both, low, high, out_1, out_2, flat = call(
        first_kernel_body,
        [
            ((height, 2 * hid, 128), BF), ((2 * hid, 128), BF), ((2 * hid, 128), BF),
            ((2, 2 * hid, 128), BF), ((2, 2 * hid, 128), BF), ((rows * devices, 128), WIRE),
        ],
        [
            ((height, 5 * CP, 128), BF), ((height, 5 * CP, 128), BF),
            ((height + 8, hid, 128), F32), ((height + 8, hid, 128), F32),
            ((height + 8, hid, 128), BF), ((height + 8, hid, 128), BF),
            ((4, 5 * CP, 128), BF), ((4, 5 * CP, 128), BF),
            ((5 * CP, 256), BF), ((5 * CP, 256), BF),
            ((2, hid, 128), F32), ((2, hid, 128), F32),
        ],
        (
            numbers, main, right, left, rim_1, rim_2, far_1, far_2, w_1, w_2, spread,
        ),
        12 * us,
        48,
    )

    got = lax.all_to_all(flat.reshape(devices, rows, 128), AXES, 0, 0)
    right, left = exchange_columns(low, high)
    sides = jnp.stack([right, left], axis=0)
    out_1, far_1 = lax.ppermute((out_1, sides), AXES, one)
    out_2, far_2 = lax.ppermute((out_2, sides), AXES, two)
    factor = (height * width * devices) ** -0.5
    (mine,) = call(
        functools.partial(reduce_kernel, factor), [((devices, rows, 128), BF)], [],
        (numbers, got),
        10 * us,
        8,
    )
    mine, out_1, out_2, far_1, far_2 = lax.optimization_barrier((mine, out_1, out_2, far_1, far_2))
    summed = lax.all_to_all(mine, AXES, 0, 0).reshape(-1, 128)
    grad_1, grad_2, gain = call(
        unpack_kernel,
        [((5, 5, hid, channels), F32)] * 2 + [((1, hid), F32)],
        [],
        (summed,),
        20 * us,
        16,
        numbers=False,
    )
    grad_first = jnp.transpose(grad_1, (2, 3, 0, 1))
    grad_second = jnp.transpose(grad_2, (3, 2, 0, 1))

    results = []
    for which, weight, base in ((0, w_3, field), (1, w_4, cotangent)):
        results += call(
            functools.partial(second_kernel_body, which),
            [(field.shape, BF)],
            [((height + 4, 5 * hid, 128), BF), ((height + 8, CP, 128), F32)],
            (numbers, both, right, left, out_1, out_2, far_1, far_2, weight, base),
            2 * us,
            36,
        )
    return results[0], results[1], grad_first, grad_second, gain.reshape(hid)


def solution(mesh):
    placed = (P(None, "lat", "lon"), P(), P(), P(), P(None, "lat", "lon"))
    return jax.shard_map(
        per_device,
        mesh=mesh,
        in_specs=placed,
        out_specs=(P(None, "lat", "lon"), P(None, "lat", "lon"), P(), P(), P()),
        check_vma=False,
    )
```
